128 devices in a mesh: blk: 64 (over z_lo, y, x, core), rows: 2 (over z_hi).
Axes of the slice: x: 4, y: 4, z: 4 (z_hi: 2, z_lo: 2; z = z_hi * 2 + z_lo), core: 2. Of those that a mesh axis runs over, the one named last changes fastest.
Arguments:
- embedding: float32 [32768, 400], P(('blk', 'rows')), may hold values from -2 to 2
- emb_state: float32 [32768], P(('blk', 'rows')), may hold values from 0.001 to 0.1
- entity_slot: int32 [32768], P(('blk', 'rows')), may hold values from 0 to 32767, as said below
- relations: float32 [256, 400], replicated, may hold values from 0.5 to 1.5
- rel_state: float32 [256], replicated, may hold values from 0.01 to 1
- edge_src: int32 [3, 65536], P(None, ('blk', 'rows')), may hold values from 0 to 511
- edge_rel: int32 [3, 65536], P(None, ('blk', 'rows')), may hold values from 0 to 255
- edge_dst: int32 [3, 65536], P(None, ('blk', 'rows')), may hold values from 0 to 511
- negatives: int32 [3, 128000], P(None, ('blk', 'rows')), may hold values from 0 to 511
- edge_count: int32 [3, 128], P(None, ('blk', 'rows')), may hold values from 1 to 512, 39321 in all within a row
Outputs:
- new_embedding: float32 [32768, 400], P(('blk', 'rows'))
- new_emb_state: float32 [32768], P(('blk', 'rows'))
- new_relations: float32 [256, 400], replicated
- new_rel_state: float32 [256], replicated
The draws below stay inside these ranges and needn't reach their ends.
Inputs may be any that keep to these rules, and one draw needn't show every extreme that they name: entity_slot is a permutation; the 256 entities of each device in row-owner order land exactly 2 on each device's rows in partition order (position // 256 is that device). `edge_count`: in every step some device has all 512 slots live.
All inputs are finite; a program needn't handle non-finite values.
Results may differ from the reference program's by a relative error of at most 0.0003.
Values sent between devices are 32-bit elements; how exact they have to be, the bound alone decides.
No kernel may reach another device: no remote copies, remote signals or barrier semaphores. Data moves between devices by JAX's collectives and lax.ppermute only.
A program may use at most 128 MiB of HBM per device.

```python
import math
import jax
import jax.numpy as jnp
import numpy as np
from jax import lax

D = 400
NREL = 256
NEG = 1000
STEPS = 3
ENT_DEV = 256
CAP = 512
PART = 512
ENT = 32768
EDGES = 65536
N_BLK = 64
N_ROWS = 2
DEVICES = 128


def draw_entity_slot(key, part):
    key = jax.random.fold_in(key, 11)
    devices = ENT // ENT_DEV
    share = ENT_DEV // devices
    first, second = jax.random.split(key)
    pair_perm = jax.vmap(lambda k: jax.random.permutation(k, ENT_DEV))(jax.random.split(first, devices))
    target = pair_perm // share
    layer = pair_perm % share
    source = jnp.arange(devices, dtype=jnp.int32)[:, None]
    begin = layer * devices + source
    place_perm = jax.vmap(lambda k: jax.random.permutation(k, ENT_DEV))(jax.random.split(second, devices))
    position = place_perm[target, begin]
    return (target * ENT_DEV + position).reshape(-1).astype(jnp.int32)


def plant(result, rng, least, largest):
    place = [jax.random.randint(jax.random.fold_in(rng, axis), (), 0, length) for axis, length in enumerate(result.shape)]
    longest = result.shape.index(max(result.shape))
    beside = place[:longest] + [(place[longest] + 1) % result.shape[longest]] + place[longest + 1:]
    return result.at[tuple(place)].set(least).at[tuple(beside)].set(largest)


def block_scale(key, extent, shards, least, top_value):
    level, own = 1.0, jax.random.fold_in(key, 6)
    for dim, parts in shards:
        draws = jnp.exp(jax.random.uniform(jax.random.fold_in(own, dim), (parts,), jnp.float32, least / len(shards), top_value / len(shards)))
        level = level * jnp.repeat(draws, extent[dim] // parts).reshape([-1 if axis == dim else 1 for axis in range(len(extent))])
    return level


def cumulative_ranks(number_of, slope):
    weights = [(1 << 20) // math.isqrt(standing ** slope) + 1 for standing in range(1, number_of + 1)]
    deviation = 1 + sum(weights) // (1 << 30)
    return np.cumsum(np.array([max(1, weight // deviation) for weight in weights]))


def skewed_ids(rng, dims, number_of, skew):
    grid = cumulative_ranks(number_of, skew)
    pick = jax.random.randint(jax.random.fold_in(rng, 1), dims, 0, int(grid[number_of - 1]))
    grade = jnp.searchsorted(jnp.asarray(grid, jnp.int32), pick, side="right")
    return jax.random.permutation(jax.random.fold_in(rng, 2), number_of)[grade].astype(jnp.int32)


def split_up(amount, total, bound, skew):
    weights = [(1 << 20) // math.isqrt(rank ** skew) + 1 for rank in range(2, amount + 1)]
    surplus, given = total - bound - (amount - 1), [1] * (amount - 1)
    while surplus > 0:
        movable = [i for i in range(amount - 1) if given[i] < bound]
        pool, left = sum([weights[i] for i in movable]), surplus
        for i in movable:
            extra = min(bound - given[i], max(1, left * weights[i] // pool), surplus)
            given[i] = given[i] + extra
            surplus = surplus - extra
    return np.array([bound] + given)


def uneven_parts(own_key, count, total, bound, skew):
    if count == 2:
        one = jax.random.randint(own_key, (), max(1, total - bound), min(bound, total - 1) + 1)
        return jnp.stack([one, total - one])
    lengths = jnp.asarray(split_up(count, total, bound, skew), jnp.int32)
    couples = (count - 1) // 2
    source_of, sink = lengths[1:1 + 2 * couples:2], lengths[2:2 + 2 * couples:2]
    room = jnp.minimum(source_of - 1, bound - sink)
    passed = jax.random.randint(jax.random.fold_in(own_key, 1), (couples,), 0, 1 << 20) % (room + 1)
    lengths = lengths.at[1:1 + 2 * couples:2].set(source_of - passed).at[2:2 + 2 * couples:2].set(sink + passed)
    return lengths[jax.random.permutation(jax.random.fold_in(own_key, 2), count)]


def normal_values(key, extent, spread, limit, shards=(), held_as=jnp.bfloat16):
    values = jax.random.normal(key, extent, jnp.float32) * spread
    if len(shards) > 0:
        values = block_scale(key, extent, shards, -0.22, 0.18) * values
    return jnp.clip(values, min=-limit, max=limit).astype(held_as)


def setup_inputs(seed: int = 0) -> dict:
    seeds = jax.random.split(jax.random.key(seed), 11)
    embedding = normal_values(seeds[0], (ENT, D), 0.3, 2.0, ((0, 128),), jnp.float32)
    emb_state = jnp.clip(jnp.exp(math.log(0.1) - 4.6051702 * jax.random.uniform(seeds[1], (ENT,), jnp.float32) ** block_scale(seeds[1], (ENT,), ((0, 128),), -0.2, 0.2)), 0.001, 0.1)
    entity_slot = draw_entity_slot(jax.random.fold_in(seeds[10], 71), 0)
    relations = jnp.clip(jax.random.uniform(seeds[3], (NREL, D), jnp.float32, 0.5, 1.5), 0.5, 1.5)
    rel_state = jnp.clip(jnp.exp(jax.random.uniform(seeds[4], (NREL,), jnp.float32, math.log(0.01), math.log(1.0))), 0.01, 1.0)
    edge_src = plant(jax.random.randint(seeds[5], (STEPS, EDGES), 0, PART), jax.random.fold_in(seeds[5], 1), 0, PART - 1).astype(jnp.int32)
    edge_rel = plant(skewed_ids(seeds[6], (STEPS, EDGES), NREL, 2), jax.random.fold_in(seeds[6], 3), 0, NREL - 1).astype(jnp.int32)
    edge_dst = plant(jax.random.randint(seeds[7], (STEPS, EDGES), 0, PART), jax.random.fold_in(seeds[7], 1), 0, PART - 1).astype(jnp.int32)
    negatives = plant(jax.random.randint(seeds[8], (STEPS, DEVICES * NEG), 0, PART), jax.random.fold_in(seeds[8], 1), 0, PART - 1).astype(jnp.int32)
    edge_count = jax.vmap(lambda own: uneven_parts(own, DEVICES, DEVICES * CAP * 3 // 5, CAP, 2))(jax.random.split(seeds[9], STEPS)).reshape((STEPS, DEVICES)).astype(jnp.int32)
    return dict(embedding=embedding, emb_state=emb_state, entity_slot=entity_slot, relations=relations, rel_state=rel_state, edge_src=edge_src, edge_rel=edge_rel, edge_dst=edge_dst, negatives=negatives, edge_count=edge_count)


learn_rate = 0.1
highest = lax.Precision.HIGHEST

def bucket_terms(lhs, rhs, rel_table, src, rel, dst, neg, count):
    cap = src.shape[0]
    nrel = rel_table.shape[0]
    nneg = neg.shape[0]
    live = (jnp.arange(cap, dtype=jnp.int32) < count).astype(jnp.float32)
    onehot = (rel[:, None] == jnp.arange(nrel, dtype=jnp.int32)[None, :]).astype(jnp.float32)
    ops = jnp.dot(onehot, rel_table, precision=highest)
    head = lhs[src]
    tail = rhs[dst]
    noise = rhs[neg]
    joined = head * ops
    pos = lax.optimization_barrier(jnp.sum(joined * tail, axis=1))
    negs = lax.dot_general(joined, noise, (((1,), (1,)), ((), ())), precision=highest)
    coef = -live * jax.nn.sigmoid(-pos)
    weight = live[:, None] * jax.nn.sigmoid(negs) / nneg
    g_joined = coef[:, None] * tail + jnp.dot(weight, noise, precision=highest)
    g_head = g_joined * ops
    g_tail = coef[:, None] * joined
    g_noise = lax.dot_general(weight, joined, (((0,), (0,)), ((), ())), precision=highest)
    g_rel = lax.dot_general(onehot, g_joined * head, (((0,), (0,)), ((), ())), precision=highest)
    lhs_grad = jnp.zeros(lhs.shape, jnp.float32).at[src].add(g_head)
    rhs_grad = jnp.zeros(rhs.shape, jnp.float32).at[dst].add(g_tail).at[neg].add(g_noise)
    return (lhs_grad, rhs_grad, g_rel)

def reference(embedding, emb_state, entity_slot, relations, rel_state, edge_src, edge_rel, edge_dst, negatives, edge_count):
    part = ENT_DEV * N_ROWS
    devices = N_BLK * N_ROWS
    part_emb = jnp.zeros(embedding.shape, jnp.float32).at[entity_slot].set(embedding)
    total = STEPS * devices
    srcs = edge_src.reshape(total, CAP)
    rels = edge_rel.reshape(total, CAP)
    dsts = edge_dst.reshape(total, CAP)
    negs = negatives.reshape(total, NEG)
    counts = edge_count.reshape(total)
    index = jnp.arange(total, dtype=jnp.int32)

    def visit(carry, item):
        grad, rgrad = carry
        idx, src, rel, dst, neg, count = item
        step = idx // devices
        owner = idx % devices // N_ROWS
        right = (owner - step) % N_BLK
        lstart = (owner * part).astype(jnp.int32)
        rstart = (right * part).astype(jnp.int32)
        lhs = lax.dynamic_slice_in_dim(part_emb, lstart, part, 0)
        rhs = lax.dynamic_slice_in_dim(part_emb, rstart, part, 0)
        lg, rg, relg = bucket_terms(lhs, rhs, relations, src, rel, dst, neg, count)
        grad = lax.dynamic_update_slice_in_dim(grad, lax.dynamic_slice_in_dim(grad, lstart, part, 0) + lg, lstart, 0)
        grad = lax.dynamic_update_slice_in_dim(grad, lax.dynamic_slice_in_dim(grad, rstart, part, 0) + rg, rstart, 0)
        return ((grad, rgrad + relg), None)
    start = (jnp.zeros(embedding.shape, jnp.float32), jnp.zeros(relations.shape, jnp.float32))
    (grad_part, grad_rel), _ = lax.scan(visit, start, (index, srcs, rels, dsts, negs, counts))
    grad_owner = grad_part[entity_slot]
    new_emb_state = emb_state + lax.optimization_barrier(jnp.mean(grad_owner * grad_owner, axis=1))
    new_embedding = embedding - learn_rate * grad_owner / jnp.sqrt(new_emb_state)[:, None]
    new_rel_state = rel_state + lax.optimization_barrier(jnp.mean(grad_rel * grad_rel, axis=1))
    new_relations = relations - learn_rate * grad_rel / jnp.sqrt(new_rel_state)[:, None]
    return (new_embedding, new_emb_state, new_relations, new_rel_state)
```

```python
import jax
import jax.numpy as jnp
from jax import lax
from jax.experimental import pallas as pl
from jax.experimental.pallas import tpu as pltpu
from jax.sharding import PartitionSpec as P

learn_rate = 0.1
axes = ("blk", "rows")
devices = 128
chips = 64
part = 512
half = 256
width = 400
wide = 512
nrel = 256
cap = 512
nneg = 1000
steps = 3
edge_rows = 24
f32 = jnp.float32
bf16 = jnp.bfloat16


def device_at(place, core):
    run, offset = place // 4, place % 4
    z, turn = run // 4, run % 4
    y = (turn - z) % 4
    x = (offset - run) % 4
    block = (((z % 2) * 4 + y) * 4 + x) * 2 + core
    return block * 2 + z // 2


def half_of_device(index):
    block, z_hi = index >> 1, index & 1
    core, x, y, z_lo = block & 1, (block >> 1) & 3, (block >> 3) & 3, block >> 5
    z = 2 * z_hi + z_lo
    turn = (y + z) & 3
    place = 16 * z + 4 * turn + ((x + turn) & 3)
    return 2 * place + core


def every(source, target):
    return [(source(p, h), target(p, h)) for p in range(chips) for h in range(2)]


swap_cores = every(device_at, lambda p, h: device_at(p, 1 - h))
go_up = every(device_at, lambda p, h: device_at((p + 1) % chips, h))
go_down = every(device_at, lambda p, h: device_at((p - 1) % chips, h))
edges_here = every(lambda p, h: 2 * p + h, device_at)
edges_next = every(lambda p, h: 2 * ((p + 1) % chips) + h, device_at)


def sent(value, pairs):
    return lax.ppermute(value, axes, pairs)


def exchanged(value):
    return lax.all_to_all(value, axes, split_axis=0, concat_axis=0, tiled=True)


def two(value):
    high = value.astype(bf16)
    return high, (value - high.astype(f32)).astype(bf16)


def three(value):
    high = value.astype(bf16)
    rest = value - high.astype(f32)
    mid = rest.astype(bf16)
    return high, mid, (rest - mid.astype(f32)).astype(bf16)


def mm(a, b, contract=(1, 0)):
    return lax.dot_general(
        a, b, (((contract[0],), (contract[1],)), ((), ())), preferred_element_type=f32
    )


def mm3(a, b, contract=(1, 0)):
    return (mm(a[0], b[1], contract) + mm(a[1], b[0], contract)) + mm(a[0], b[0], contract)


def lane_iota(shape):
    return lax.broadcasted_iota(jnp.int32, shape, len(shape) - 1)


def start_kernel(slot_ref, emb_ref, src_ref, rel_ref, dst_ref, neg_ref, count_ref, send_ref, perm_ref, edge_ref, last_ref):
    slot = slot_ref[...]
    owner = half_of_device(lax.broadcasted_iota(jnp.int32, (devices, half), 0))
    match = owner == (slot >> 8)
    before = (
        lax.broadcasted_iota(jnp.int32, (half, half), 0) < lane_iota((half, half))
    ).astype(f32).astype(bf16)
    earlier = mm(match.astype(f32).astype(bf16), before)
    place = (slot & (part - 1)).astype(f32)
    last_ref[...] = jnp.zeros(last_ref.shape, f32)
    last_ref[:, : width - 384] = emb_ref[:, 384:]
    for layer in range(2):
        pick = jnp.where(match, jnp.where(jnp.abs(earlier - layer) < 0.5, 1.0, 0.0), 0.0)
        places = jnp.sum(pick * place, axis=1, keepdims=True)
        pick = pick.astype(bf16)
        perm_ref[layer * devices : (layer + 1) * devices, :] = pick
        for c in range(4):
            rows = emb_ref[:, c * 128 : (c + 1) * 128] if c < 3 else last_ref[...]
            high, mid, low = three(rows)
            out = mm(pick, high) + (mm(pick, mid) + mm(pick, low))
            if c == 3:
                out = jnp.where(lane_iota(out.shape) == width - 384, places, out)
            send_ref[pl.ds(layer * 4 + c, devices, stride=8), :] = out
    for s in range(steps):
        base = s * edge_rows
        for j in range(4):
            lanes = slice(j * 128, (j + 1) * 128)
            edge_ref[base + j : base + j + 1, :] = src_ref[s : s + 1, lanes].astype(f32)
            edge_ref[base + 4 + j : base + 5 + j, :] = rel_ref[s : s + 1, lanes].astype(f32)
            edge_ref[base + 8 + j : base + 9 + j, :] = dst_ref[s : s + 1, lanes].astype(f32)
        edge_ref[base + 19 : base + 20, :] = jnp.full((1, 128), -1.0, f32)
        for j in range(8):
            end = min((j + 1) * 128, nneg)
            edge_ref[base + 12 + j : base + 13 + j, : end - j * 128] = neg_ref[
                s : s + 1, j * 128 : end
            ].astype(f32)
        edge_ref[base + 20 : base + edge_rows, :] = jnp.broadcast_to(
            count_ref[s : s + 1, :].astype(f32), (edge_rows - 20, 128)
        )


def load_part(refs):
    blocks = []
    for c in range(4):
        blocks.append(
            jnp.concatenate(
                [ref[pl.ds(layer * 4 + c, devices, stride=8), :] for ref in refs for layer in range(2)],
                axis=0,
            )
        )
    last = blocks[3]
    mark = width - 384
    column = last[:, mark : mark + 1]
    row = last.T[mark : mark + 1, :]
    blocks[3] = jnp.where(lane_iota(last.shape) < mark, last, 0.0)
    full = jnp.concatenate(blocks, axis=1)
    return two(full), row, column


def onehot(a, b):
    return jnp.where(a == b, 1.0, 0.0).astype(bf16)


def unit(lhs, rhs, rel, edges):
    (lh, ll), lrow, lcol = lhs
    rhs_two, rrow, _ = rhs
    flipped = edges.T
    row = lambda first: jnp.concatenate([edges[first + j : first + j + 1, :] for j in range(4)], axis=1)
    column = lambda first, n: jnp.concatenate([flipped[:, first + j : first + j + 1] for j in range(n)], axis=0)
    src_row, src_col = row(0), column(0, 4)
    rel_row, rel_col = row(4), column(4, 4)
    dst_col, neg_col = column(8, 4), column(12, 8)
    count = edges[20:21, 0:1]
    pick_src = onehot(src_col, lrow)
    pick_rel = onehot(rel_col, lane_iota((cap, nrel)).astype(f32))
    put_src = onehot(lcol, src_row)
    put_rel = onehot(lax.broadcasted_iota(jnp.int32, (nrel, cap), 0).astype(f32), rel_row)
    at_dst = dst_col == rrow
    times = jnp.sum(jnp.where(neg_col == rrow, 1.0, 0.0), axis=0, keepdims=True) * (1.0 / nneg)
    live = lax.broadcasted_iota(jnp.int32, (cap, 1), 0).astype(f32) < count
    head = mm(pick_src, ll) + mm(pick_src, lh)
    ops = mm(pick_rel, rel[1]) + mm(pick_rel, rel[0])
    joined = two(head * ops)
    scores = mm3(joined, rhs_two, (1, 1))
    pos = jnp.sum(jnp.where(at_dst, scores, 0.0), axis=1, keepdims=True)
    coef = jax.nn.sigmoid(-pos)
    weight = times * (0.5 + 0.5 * jnp.tanh(0.5 * scores)) - jnp.where(at_dst, coef, 0.0)
    weight = two(jnp.where(live, weight, 0.0))
    g_joined = mm3(weight, rhs_two)
    rhs_grad = mm3(weight, joined, (0, 0))
    gh, gl = two(g_joined * ops)
    lhs_grad = mm(put_src, gl) + mm(put_src, gh)
    gh, gl = two(g_joined * head)
    rel_grad = mm(put_rel, gl) + mm(put_rel, gh)
    return lhs_grad, rhs_grad, rel_grad


def load_rel(rel_ref, pad_ref):
    pad_ref[:, 384:] = jnp.zeros((nrel, 128), f32)
    pad_ref[:, :width] = rel_ref[...]
    return two(pad_ref[...])


def store_half(ref, grad, which):
    for layer in range(2):
        begin = which * half + layer * devices
        for c in range(4):
            ref[pl.ds(layer * 4 + c, devices, stride=8), :] = grad[
                begin : begin + devices, c * 128 : (c + 1) * 128
            ]


def first_kernel(own_ref, mate_ref, rel_ref, edge_ref, grad_ref, grel_ref, pad_ref):
    mine = load_part((own_ref, mate_ref))
    rel = load_rel(rel_ref, pad_ref)
    lg, rg, relg = unit(mine, mine, rel, edge_ref[:edge_rows, :])
    grad_ref[...] = lg + rg
    grel_ref[...] = relg


def second_kernel(
    own_ref, mate_ref, down_ref, down_mate_ref, up_ref, up_mate_ref, rel_ref, edge_ref, next_ref, grad_ref, grel_ref,
    down_keep, down_give, up_keep, up_give, own_keep, own_give, rel_out, pad_ref,
):
    mine = load_part((own_ref, mate_ref))
    below = load_part((down_ref, down_mate_ref))
    above = load_part((up_ref, up_mate_ref))
    rel = load_rel(rel_ref, pad_ref)
    ug, dg, rel2 = unit(above, below, rel, next_ref[...])
    store_half(up_keep, ug, 0)
    store_half(up_give, ug, 1)
    lg, rg, rel1 = unit(mine, below, rel, edge_ref[edge_rows : 2 * edge_rows, :])
    lg = lg + grad_ref[...]
    dg = dg + rg
    store_half(down_keep, dg, 0)
    store_half(down_give, dg, 1)
    store_half(own_keep, lg, 0)
    store_half(own_give, lg, 1)
    relg = grel_ref[...] + rel1 + rel2
    for c in range(4):
        rel_out[pl.ds(c, nrel, stride=4), :] = relg[:, c * 128 : (c + 1) * 128]


def gather_kernel(keep_ref, give_ref, up_ref, down_ref, rel_ref, out_ref):
    out_ref[:, :8, :] = (keep_ref[...] + give_ref[...]) + (up_ref[...] + down_ref[...])
    out_ref[:, 8:, :] = jnp.broadcast_to(jnp.sum(rel_ref[...], axis=0, keepdims=True), (devices, 8, 128))


def update(grads, value_ref, state_ref, new_value_ref, new_state_ref):
    total = sum(jnp.sum(g * g, axis=1, keepdims=True) for g in grads)
    state = jnp.broadcast_to(state_ref[...], (128, half)).T[:, 0:1]
    state = state + total * (1.0 / width)
    new_state_ref[...] = jnp.broadcast_to(state, (half, 128)).T[0:1, :]
    scale = learn_rate / jnp.sqrt(state)
    for c in range(4):
        begin, end = c * 128, min((c + 1) * 128, width)
        new_value_ref[:, begin:end] = value_ref[:, begin:end] - scale * grads[c][:, : end - begin]


def finish_kernel(
    got_ref, perm_ref, emb_ref, state_ref, rel_ref, rel_state_ref, new_emb_ref, new_state_ref, new_rel_ref, new_rel_state_ref,
    order_ref, rel_grad_ref,
):
    perm = perm_ref[...]
    grads = []
    for c in range(4):
        rows = jnp.concatenate([got_ref[pl.ds(layer * 4 + c, devices, stride=16), :] for layer in range(2)], axis=0)
        high, mid, low = three(rows)
        grads.append(mm(perm, high, (0, 0)) + (mm(perm, mid, (0, 0)) + mm(perm, low, (0, 0))))
    update(grads, emb_ref, state_ref, new_emb_ref, new_state_ref)
    for c in range(4):
        for t in range(2):
            order_ref[pl.ds(t, devices, stride=2), :] = got_ref[pl.ds(8 + t * 4 + c, devices, stride=16), :]
        rel_grad_ref[:, c * 128 : (c + 1) * 128] = order_ref[...]
    rel_grads = [rel_grad_ref[:, c * 128 : (c + 1) * 128] for c in range(4)]
    update(rel_grads, rel_ref, rel_state_ref, new_rel_ref, new_rel_state_ref)


def call(kernel, outs, scratch=(), flops=0):
    return pl.pallas_call(
        kernel,
        out_shape=[jax.ShapeDtypeStruct(shape, dtype) for shape, dtype in outs],
        scratch_shapes=[pltpu.VMEM(shape, f32) for shape in scratch],
        compiler_params=pltpu.CompilerParams(vmem_limit_bytes=48 * 1024 * 1024),
        cost_estimate=pl.CostEstimate(flops=flops, bytes_accessed=4 << 20, transcendentals=0),
    )


def per_device(
    embedding,
    emb_state,
    entity_slot,
    relations,
    rel_state,
    edge_src,
    edge_rel,
    edge_dst,
    negatives,
    edge_count,
):
    flat = (devices * 8, 128)
    blocks = (devices, 8, 128)
    send, perm, edges = call(
        start_kernel,
        [(flat, f32), ((half, half), bf16), ((steps * edge_rows, 128), f32)],
        [(half, 128)],
    )(entity_slot.reshape(1, half), embedding, edge_src, edge_rel, edge_dst, negatives, edge_count)
    here = sent(edges[: 2 * edge_rows], edges_here)
    following = sent(edges[2 * edge_rows :], edges_next)
    own = exchanged(send.reshape(blocks)).reshape(flat)
    mate = sent(own, swap_cores)
    down = sent(own, go_up)
    up = sent(own, go_down)
    grad, grel = call(
        first_kernel,
        [((part, wide), f32), ((nrel, wide), f32)],
        [(nrel, wide)],
        6 << 30,
    )(own, mate, relations, here)
    down_mate = sent(down, swap_cores)
    up_mate = sent(up, swap_cores)
    down_keep, down_give, up_keep, up_give, own_keep, own_give, rel_part = call(
        second_kernel, [(flat, f32)] * 7, [(nrel, wide)], 12 << 30
    )(own, mate, down, down_mate, up, up_mate, relations, here, following, grad, grel)
    down_sum = down_keep + sent(down_give, swap_cores)
    up_sum = up_keep + sent(up_give, swap_cores)
    own_got = sent(own_give, swap_cores)
    from_up = sent(down_sum, go_down)
    from_down = sent(up_sum, go_up)
    rel_got = exchanged(rel_part.reshape(blocks))
    (back,) = call(gather_kernel, [((devices, 16, 128), f32)])(
        own_keep.reshape(blocks), own_got.reshape(blocks), from_up.reshape(blocks), from_down.reshape(blocks), rel_got
    )
    got = exchanged(back).reshape(devices * 16, 128)
    new_embedding, new_state, new_relations, new_rel_state = call(
        finish_kernel,
        [((half, width), f32), ((1, half), f32), ((nrel, width), f32), ((1, nrel), f32)],
        [(nrel, 128), (nrel, wide)],
    )(got, perm, embedding, emb_state.reshape(1, half), relations, rel_state.reshape(1, nrel))
    return (
        new_embedding,
        new_state.reshape(half),
        new_relations,
        new_rel_state.reshape(nrel),
    )


def solution(mesh):
    placed = (
        P(axes, None),
        P(axes),
        P(axes),
        P(),
        P(),
        P(None, axes),
        P(None, axes),
        P(None, axes),
        P(None, axes),
        P(None, axes),
    )
    return jax.shard_map(
        per_device,
        mesh=mesh,
        in_specs=placed,
        out_specs=(P(axes, None), P(axes), P(), P()),
        check_vma=False,
    )
```

```python
import jax
import jax.numpy as jnp
from jax import lax
from jax.experimental import pallas as pl
from jax.experimental.pallas import tpu as pltpu
from jax.sharding import PartitionSpec as P

learn_rate = 0.1
axes = ("blk", "rows")
devices = 128
chips = 64
part = 512
half = 256
width = 400
wide = 512
nrel = 256
cap = 512
nneg = 1000
steps = 3
edge_rows = 24
f32 = jnp.float32
bf16 = jnp.bfloat16


def device_at(place, core):
    visit, y, step = place // 32, place // 8 % 4, place % 8
    x = step if step < 4 else 7 - step
    odd = (y % 2) if step < 4 else 1 - y % 2
    z = 2 * visit + odd if y < 3 or odd else (2 * visit + 2) % 4
    block = (((z % 2) * 4 + y) * 4 + x) * 2 + core
    return block * 2 + z // 2


def half_of_device(index):
    block, z_hi = index >> 1, index & 1
    core, x, y, z_lo = block & 1, (block >> 1) & 3, (block >> 3) & 3, block >> 5
    z = 2 * z_hi + z_lo
    visit = jnp.where(y == 3, 1 - (((z + 1) >> 1) & 1), z >> 1)
    step = jnp.where((z & 1) == (y & 1), x, 7 - x)
    return 2 * (32 * visit + 8 * y + step) + core


def every(source, target):
    return [(source(p, h), target(p, h)) for p in range(chips) for h in range(2)]


swap_cores = every(device_at, lambda p, h: device_at(p, 1 - h))
go_up = every(device_at, lambda p, h: device_at((p + 1) % chips, h))
go_down = every(device_at, lambda p, h: device_at((p - 1) % chips, h))
edges_next = every(lambda p, h: 2 * ((p + 1) % chips) + h, device_at)
edges_here = every(lambda p, h: 2 * p + h, device_at)


def sent(value, pairs):
    return lax.ppermute(value, axes, pairs)


def exchanged(value):
    return lax.all_to_all(value, axes, split_axis=0, concat_axis=0, tiled=True)


def two(value):
    high = value.astype(bf16)
    return high, (value - high.astype(f32)).astype(bf16)


def three(value):
    high = value.astype(bf16)
    rest = value - high.astype(f32)
    mid = rest.astype(bf16)
    return high, mid, (rest - mid.astype(f32)).astype(bf16)


def mm(a, b, contract=(1, 0)):
    return lax.dot_general(
        a, b, (((contract[0],), (contract[1],)), ((), ())), preferred_element_type=f32
    )


def mm3(a, b, contract=(1, 0)):
    return (mm(a[0], b[1], contract) + mm(a[1], b[0], contract)) + mm(a[0], b[0], contract)


def lane_iota(shape):
    return lax.broadcasted_iota(jnp.int32, shape, len(shape) - 1)


def start_kernel(*refs):
    far, (send_ref, perm_ref, edge_ref), near = refs[:7], refs[7:10], refs[10:17]
    last_ref, arrived = refs[17:]
    copies = [pltpu.make_async_copy(a, b, arrived.at[i]) for i, (a, b) in enumerate(zip(far, near))]
    for copy in copies:
        copy.start()
    slot_ref, emb_ref, src_ref, rel_ref, dst_ref, neg_ref, count_ref = near
    copies[0].wait()
    slot = slot_ref[...]
    owner = half_of_device(lax.broadcasted_iota(jnp.int32, (devices, half), 0))
    match = owner == (slot >> 8)
    before = (
        lax.broadcasted_iota(jnp.int32, (half, half), 0) < lane_iota((half, half))
    ).astype(f32).astype(bf16)
    earlier = mm(match.astype(f32).astype(bf16), before)
    last_ref[...] = jnp.zeros(last_ref.shape, f32)
    copies[1].wait()
    last_ref[: width - 384, :] = emb_ref[384:, :]
    last_ref[width - 384 : width - 383, :] = (slot & (part - 1)).astype(f32)
    pieces = [three(emb_ref[c * 128 : (c + 1) * 128, :] if c < 3 else last_ref[...]) for c in range(4)]
    for layer in range(2):
        pick = jnp.where(match, jnp.where(jnp.abs(earlier - layer) < 0.5, 1.0, 0.0), 0.0).astype(bf16)
        perm_ref[layer * devices : (layer + 1) * devices, :] = pick
        for c in range(4):
            high, mid, low = pieces[c]
            out = mm(pick, high, (1, 1)) + (mm(pick, mid, (1, 1)) + mm(pick, low, (1, 1)))
            send_ref[pl.ds(layer * 4 + c, devices, stride=8), :] = out
    for copy in copies[2:]:
        copy.wait()
    for s in range(steps):
        base = s * edge_rows
        for j in range(4):
            lanes = slice(j * 128, (j + 1) * 128)
            edge_ref[base + j : base + j + 1, :] = src_ref[s : s + 1, lanes].astype(f32)
            edge_ref[base + 4 + j : base + 5 + j, :] = rel_ref[s : s + 1, lanes].astype(f32)
            edge_ref[base + 8 + j : base + 9 + j, :] = dst_ref[s : s + 1, lanes].astype(f32)
        edge_ref[base + 19 : base + 20, :] = jnp.full((1, 128), -1.0, f32)
        for j in range(8):
            end = min((j + 1) * 128, nneg)
            edge_ref[base + 12 + j : base + 13 + j, : end - j * 128] = neg_ref[
                s : s + 1, j * 128 : end
            ].astype(f32)
        edge_ref[base + 20 : base + edge_rows, :] = jnp.broadcast_to(
            count_ref[:, s : s + 1].astype(f32), (edge_rows - 20, 128)
        )


def load_part(refs):
    blocks = []
    for c in range(4):
        blocks.append(
            jnp.concatenate(
                [ref[pl.ds(layer * 4 + c, devices, stride=8), :] for ref in refs for layer in range(2)],
                axis=0,
            )
        )
    last = blocks[3]
    mark = width - 384
    column = last[:, mark : mark + 1]
    row = last.T[mark : mark + 1, :]
    blocks[3] = jnp.where(lane_iota(last.shape) < mark, last, 0.0)
    full = jnp.concatenate(blocks, axis=1)
    return two(full), row, column


def onehot(a, b):
    return jnp.where(a == b, 1.0, 0.0).astype(bf16)


def unit(lhs, rhs, rel, edges):
    (lh, ll), lrow, lcol = lhs
    rhs_two, rrow, _ = rhs
    flipped = edges.T
    row = lambda first: jnp.concatenate([edges[first + j : first + j + 1, :] for j in range(4)], axis=1)
    column = lambda first, n: jnp.concatenate([flipped[:, first + j : first + j + 1] for j in range(n)], axis=0)
    src_row, src_col = row(0), column(0, 4)
    rel_row, rel_col = row(4), column(4, 4)
    dst_col, neg_col = column(8, 4), column(12, 8)
    count = edges[20:21, 0:1]
    pick_src = onehot(src_col, lrow)
    pick_rel = onehot(rel_col, lane_iota((cap, nrel)).astype(f32))
    put_src = onehot(lcol, src_row)
    put_rel = onehot(lax.broadcasted_iota(jnp.int32, (nrel, cap), 0).astype(f32), rel_row)
    at_dst = dst_col == rrow
    times = jnp.sum(jnp.where(neg_col == rrow, 1.0, 0.0), axis=0, keepdims=True) * (1.0 / nneg)
    live = lax.broadcasted_iota(jnp.int32, (cap, 1), 0).astype(f32) < count
    head = mm(pick_src, ll) + mm(pick_src, lh)
    ops = mm(pick_rel, rel[1], (1, 1)) + mm(pick_rel, rel[0], (1, 1))
    joined = two(head * ops)
    scores = mm3(joined, rhs_two, (1, 1))
    pos = jnp.sum(jnp.where(at_dst, scores, 0.0), axis=1, keepdims=True)
    coef = jax.nn.sigmoid(-pos)
    weight = times * (0.5 + 0.5 * jnp.tanh(0.5 * scores)) - jnp.where(at_dst, coef, 0.0)
    weight = two(jnp.where(live, weight, 0.0))
    g_joined = mm3(weight, rhs_two)
    rhs_grad = mm3(weight, joined, (0, 0))
    gh, gl = two(g_joined * ops)
    lhs_grad = mm(put_src, gl) + mm(put_src, gh)
    gh, gl = two(g_joined * head)
    rel_grad = mm(put_rel, gl) + mm(put_rel, gh)
    return lhs_grad, rhs_grad, rel_grad


def load_rel(rel_ref, pad_ref):
    pad_ref[384:, :] = jnp.zeros((128, nrel), f32)
    pad_ref[:width, :] = rel_ref[...]
    return two(pad_ref[...])


def store_half(ref, grad, which):
    for layer in range(2):
        begin = which * half + layer * devices
        for c in range(4):
            ref[pl.ds(layer * 4 + c, devices, stride=8), :] = grad[
                begin : begin + devices, c * 128 : (c + 1) * 128
            ]


def first_kernel(own_ref, mate_ref, rel_ref, edge_ref, grad_ref, grel_ref, pad_ref):
    mine = load_part((own_ref, mate_ref))
    rel = load_rel(rel_ref, pad_ref)
    lg, rg, relg = unit(mine, mine, rel, edge_ref[:edge_rows, :])
    grad_ref[...] = lg + rg
    grel_ref[...] = relg


def second_kernel(
    own_ref, mate_ref, down_ref, down_mate_ref, up_ref, up_mate_ref, rel_ref, edge_ref, next_ref, grad_ref, grel_ref,
    down_keep, down_give, up_keep, up_give, own_keep, own_give, rel_out, pad_ref,
):
    mine = load_part((own_ref, mate_ref))
    below = load_part((down_ref, down_mate_ref))
    above = load_part((up_ref, up_mate_ref))
    rel = load_rel(rel_ref, pad_ref)
    ug, dg, rel2 = unit(above, below, rel, next_ref[...])
    store_half(up_keep, ug, 0)
    store_half(up_give, ug, 1)
    lg, rg, rel1 = unit(mine, below, rel, edge_ref[edge_rows : 2 * edge_rows, :])
    lg = lg + grad_ref[...]
    dg = dg + rg
    store_half(down_keep, dg, 0)
    store_half(down_give, dg, 1)
    store_half(own_keep, lg, 0)
    store_half(own_give, lg, 1)
    relg = grel_ref[...] + rel1 + rel2
    for c in range(4):
        rel_out[pl.ds(c, nrel, stride=4), :] = relg[:, c * 128 : (c + 1) * 128]


def gather_kernel(keep_ref, give_ref, up_ref, down_ref, rel_ref, out_ref):
    out_ref[:, :8, :] = (keep_ref[...] + give_ref[...]) + (up_ref[...] + down_ref[...])
    out_ref[:, 8:, :] = jnp.broadcast_to(jnp.sum(rel_ref[...], axis=0, keepdims=True), (devices, 8, 128))


def update(grads, value_ref, state_ref, new_value_ref, new_state_ref):
    state = state_ref[...] + sum(jnp.sum(g * g, axis=0, keepdims=True) for g in grads) * (1.0 / width)
    new_state_ref[...] = state
    scale = learn_rate / jnp.sqrt(state)
    for c in range(4):
        begin, end = c * 128, min((c + 1) * 128, width)
        new_value_ref[begin:end, :] = value_ref[begin:end, :] - scale * grads[c][: end - begin, :]


def finish_kernel(
    got_ref, perm_ref, emb_ref, state_ref, rel_ref, rel_state_ref, new_emb_ref, new_state_ref, new_rel_ref, new_rel_state_ref,
    order_ref,
):
    perm = perm_ref[...]
    grads = []
    for c in range(4):
        rows = jnp.concatenate([got_ref[pl.ds(layer * 4 + c, devices, stride=16), :] for layer in range(2)], axis=0)
        high, mid, low = three(rows)
        grads.append(mm(high, perm, (0, 0)) + (mm(mid, perm, (0, 0)) + mm(low, perm, (0, 0))))
    update(grads, emb_ref, state_ref, new_emb_ref, new_state_ref)
    rel_grads = []
    for c in range(4):
        for t in range(2):
            order_ref[pl.ds(c * nrel + t, devices, stride=2), :] = got_ref[pl.ds(8 + t * 4 + c, devices, stride=16), :]
        rel_grads.append(order_ref[c * nrel : (c + 1) * nrel, :].T)
    update(rel_grads, rel_ref, rel_state_ref, new_rel_ref, new_rel_state_ref)


def call(kernel, outs, mebibytes, scratch=(), flops=0, **options):
    return pl.pallas_call(
        kernel,
        out_shape=[jax.ShapeDtypeStruct(shape, dtype) for shape, dtype in outs],
        scratch_shapes=[pltpu.VMEM(shape, f32) if isinstance(shape, tuple) else shape for shape in scratch],
        compiler_params=pltpu.CompilerParams(vmem_limit_bytes=mebibytes << 20),
        cost_estimate=pl.CostEstimate(flops=flops, bytes_accessed=1 << 10, transcendentals=0),
        **options,
    )


def per_device(
    embedding,
    emb_state,
    entity_slot,
    relations,
    rel_state,
    edge_src,
    edge_rel,
    edge_dst,
    negatives,
    edge_count,
):
    flat = (devices * 8, 128)
    blocks = (devices, 8, 128)
    embedding, relations = embedding.T, relations.T
    given = (entity_slot.reshape(1, half), embedding, edge_src, edge_rel, edge_dst, negatives, edge_count.T)
    send, perm, edges = call(
        start_kernel,
        [(flat, f32), ((half, half), bf16), ((steps * edge_rows, 128), f32)],
        60,
        [pltpu.VMEM(a.shape, a.dtype) for a in given] + [(128, half), pltpu.SemaphoreType.DMA((7,))],
        in_specs=[pl.BlockSpec(memory_space=pltpu.HBM)] * 7,
    )(*given)
    own = exchanged(send.reshape(blocks)).reshape(flat)
    here = sent(edges[: 2 * edge_rows], edges_here)
    following = sent(edges[2 * edge_rows :], edges_next)
    own, here, following = lax.optimization_barrier((own, here, following))
    down = sent(own, go_up)
    up = sent(own, go_down)
    mate = sent(own, swap_cores)
    grad, grel = call(
        first_kernel,
        [((part, wide), f32), ((nrel, wide), f32)],
        24,
        [(wide, nrel)],
    )(own, mate, relations, here)
    down, up, grad, grel = lax.optimization_barrier((down, up, grad, grel))
    down_mate = sent(down, swap_cores)
    up_mate = sent(up, swap_cores)
    down_keep, down_give, up_keep, up_give, own_keep, own_give, rel_part = call(
        second_kernel, [(flat, f32)] * 7, 32, [(wide, nrel)], 12 << 30
    )(own, mate, down, down_mate, up, up_mate, relations, here, following, grad, grel)
    down_sum = down_keep + sent(down_give, swap_cores)
    up_sum = up_keep + sent(up_give, swap_cores)
    own_got = sent(own_give, swap_cores)
    from_up = sent(down_sum, go_down)
    from_down = sent(up_sum, go_up)
    rel_got = exchanged(rel_part.reshape(blocks))
    (back,) = call(gather_kernel, [((devices, 16, 128), f32)], 16)(
        own_keep.reshape(blocks), own_got.reshape(blocks), from_up.reshape(blocks), from_down.reshape(blocks), rel_got
    )
    got = exchanged(back).reshape(devices * 16, 128)
    new_embedding, new_state, new_relations, new_rel_state = call(
        finish_kernel,
        [((width, half), f32), ((1, half), f32), ((width, nrel), f32), ((1, nrel), f32)],
        16,
        [(4 * nrel, 128)],
    )(got, perm, embedding, emb_state.reshape(1, half), relations, rel_state.reshape(1, nrel))
    return (
        new_embedding.T,
        new_state.reshape(half),
        new_relations.T,
        new_rel_state.reshape(nrel),
    )


def solution(mesh):
    placed = (
        P(axes, None),
        P(axes),
        P(axes),
        P(),
        P(),
        P(None, axes),
        P(None, axes),
        P(None, axes),
        P(None, axes),
        P(None, axes),
    )
    return jax.shard_map(
        per_device,
        mesh=mesh,
        in_specs=placed,
        out_specs=(P(axes, None), P(axes), P(), P()),
        check_vma=False,
    )
```

```python
import jax
import jax.numpy as jnp
from jax import lax
from jax.experimental import pallas as pl
from jax.experimental.pallas import tpu as pltpu
from jax.sharding import PartitionSpec as P

learn_rate = 0.1
axes = ("blk", "rows")
devices = 128
chips = 64
part = 512
half = 256
width = 400
wide = 512
nrel = 256
cap = 512
nneg = 1000
steps = 3
edge_rows = 24
edge = 384
tail = width - edge
block_rows = 7
back_rows = 13
f32 = jnp.float32
bf16 = jnp.bfloat16


def device_at(place, core):
    visit, y, step = place // 32, place // 8 % 4, place % 8
    x = step if step < 4 else 7 - step
    odd = (y % 2) if step < 4 else 1 - y % 2
    z = 2 * visit + odd if y < 3 or odd else (2 * visit + 2) % 4
    block = (((z % 2) * 4 + y) * 4 + x) * 2 + core
    return block * 2 + z // 2


def half_of_device(index):
    block, z_hi = index >> 1, index & 1
    core, x, y, z_lo = block & 1, (block >> 1) & 3, (block >> 3) & 3, block >> 5
    z = 2 * z_hi + z_lo
    visit = jnp.where(y == 3, 1 - (((z + 1) >> 1) & 1), z >> 1)
    step = jnp.where((z & 1) == (y & 1), x, 7 - x)
    return 2 * (32 * visit + 8 * y + step) + core


def every(source, target):
    return [(source(p, h), target(p, h)) for p in range(chips) for h in range(2)]


swap_cores = every(device_at, lambda p, h: device_at(p, 1 - h))
go_up = every(device_at, lambda p, h: device_at((p + 1) % chips, h))
go_down = every(device_at, lambda p, h: device_at((p - 1) % chips, h))
edges_next = every(lambda p, h: 2 * ((p + 1) % chips) + h, device_at)
edges_here = every(lambda p, h: 2 * p + h, device_at)


def sent(value, pairs):
    return lax.ppermute(value, axes, pairs)


def exchanged(value):
    rows = value.shape[0]
    blocks = value.reshape(devices, rows // devices, 1, 128)
    return lax.all_to_all(blocks, axes, split_axis=0, concat_axis=0, tiled=True).reshape(rows, 128)


def two(value):
    high = value.astype(bf16)
    return high, (value - high.astype(f32)).astype(bf16)


def three(value):
    high = value.astype(bf16)
    rest = value - high.astype(f32)
    mid = rest.astype(bf16)
    return high, mid, (rest - mid.astype(f32)).astype(bf16)


def mm(a, b, contract=(1, 0)):
    return lax.dot_general(
        a, b, (((contract[0],), (contract[1],)), ((), ())), preferred_element_type=f32
    )


def mm3(a, b, contract=(1, 0)):
    return (mm(a[0], b[1], contract) + mm(a[1], b[0], contract)) + mm(a[0], b[0], contract)


def lane_iota(shape):
    return lax.broadcasted_iota(jnp.int32, shape, len(shape) - 1)


def start_kernel(*refs):
    far, (send_ref, perm_ref, edge_ref), near = refs[:7], refs[7:10], refs[10:17]
    last_ref, arrived = refs[17:]
    copies = [pltpu.make_async_copy(a, b, arrived.at[i]) for i, (a, b) in enumerate(zip(far, near))]
    for copy in copies:
        copy.start()
    slot_ref, emb_ref, src_ref, rel_ref, dst_ref, neg_ref, count_ref = near
    copies[0].wait()
    slot = slot_ref[...]
    owner = half_of_device(lax.broadcasted_iota(jnp.int32, (devices, half), 0))
    match = owner == (slot >> 8)
    before = (
        lax.broadcasted_iota(jnp.int32, (half, half), 0) < lane_iota((half, half))
    ).astype(f32).astype(bf16)
    earlier = mm(match.astype(f32).astype(bf16), before)
    last_ref[...] = jnp.zeros(last_ref.shape, f32)
    copies[1].wait()
    for layer in range(2):
        begin = layer * (128 + 64)
        last_ref[begin : begin + tail, :] = emb_ref[edge:, :]
        last_ref[begin + tail : begin + tail + 1, :] = (slot & (part - 1)).astype(f32)
    pieces = [three(emb_ref[c * 128 : (c + 1) * 128, :]) for c in range(3)]
    tails = 0.0
    for layer in range(2):
        pick = jnp.where(match, jnp.where(jnp.abs(earlier - layer) < 0.5, 1.0, 0.0), 0.0).astype(bf16)
        perm_ref[layer * devices : (layer + 1) * devices, :] = pick
        for c, (high, mid, low) in enumerate(pieces + [three(last_ref[layer * 128 : (layer + 1) * 128, :])]):
            out = mm(pick, high, (1, 1)) + (mm(pick, mid, (1, 1)) + mm(pick, low, (1, 1)))
            if c < 3:
                send_ref[pl.ds(layer * 3 + c, devices, stride=block_rows), :] = out
            else:
                tails = tails + out
    send_ref[pl.ds(block_rows - 1, devices, stride=block_rows), :] = tails
    for copy in copies[2:]:
        copy.wait()
    for s in range(steps):
        base = s * edge_rows
        for j in range(4):
            lanes = slice(j * 128, (j + 1) * 128)
            edge_ref[base + j : base + j + 1, :] = src_ref[s : s + 1, lanes].astype(f32)
            edge_ref[base + 4 + j : base + 5 + j, :] = rel_ref[s : s + 1, lanes].astype(f32)
            edge_ref[base + 8 + j : base + 9 + j, :] = dst_ref[s : s + 1, lanes].astype(f32)
        edge_ref[base + 19 : base + 20, :] = jnp.full((1, 128), -1.0, f32)
        for j in range(8):
            end = min((j + 1) * 128, nneg)
            edge_ref[base + 12 + j : base + 13 + j, : end - j * 128] = neg_ref[
                s : s + 1, j * 128 : end
            ].astype(f32)
        edge_ref[base + 20 : base + edge_rows, :] = jnp.broadcast_to(
            count_ref[:, s : s + 1].astype(f32), (edge_rows - 20, 128)
        )


def main_and_tails(ref, rows, firsts, lanes):
    blocks = []
    for c in range(3):
        blocks.append(
            jnp.concatenate([ref[pl.ds(first + c, devices, stride=rows), :] for first in firsts], axis=0)
        )
    last = ref[pl.ds(rows - 1, devices, stride=rows), :]
    tails = [pltpu.roll(last, (128 - lane) % 128, 1) if lane else last for lane in lanes]
    return blocks + [jnp.concatenate(tails, axis=0)]


def load_part(refs):
    halves = [main_and_tails(ref, block_rows, (0, 3), (0, 64)) for ref in refs]
    blocks = [jnp.concatenate(pair, axis=0) for pair in zip(*halves)]
    last = blocks[3]
    column = last[:, tail : tail + 1]
    row = last.T[tail : tail + 1, :]
    blocks[3] = jnp.where(lane_iota(last.shape) < tail, last, 0.0)
    full = jnp.concatenate(blocks, axis=1)
    return two(full), row, column


def onehot(a, b):
    return jnp.where(a == b, 1.0, 0.0).astype(bf16)


def edge_views(edges):
    flipped = edges.T
    row = lambda first: jnp.concatenate([edges[first + j : first + j + 1, :] for j in range(4)], axis=1)
    column = lambda first, n: jnp.concatenate([flipped[:, first + j : first + j + 1] for j in range(n)], axis=0)
    return row, column


def heads(lhs, edges):
    (high, low), row, _ = lhs
    pick = onehot(edge_views(edges)[1](0, 4), row)
    return mm(pick, low) + mm(pick, high)


def operators(rel, edges):
    high, low = rel
    pick = onehot(edge_views(edges)[1](4, 4), lane_iota((cap, nrel)).astype(f32))
    return mm(pick, low, (1, 1)) + mm(pick, high, (1, 1))


def unit(lcol, rhs, head, ops, edges):
    rhs_two, rrow, _ = rhs
    row, column = edge_views(edges)
    dst_col, neg_col = column(8, 4), column(12, 8)
    count = edges[20:21, 0:1]
    put_src = onehot(lcol, row(0))
    put_rel = onehot(lax.broadcasted_iota(jnp.int32, (nrel, cap), 0).astype(f32), row(4))
    at_dst = dst_col == rrow
    times = jnp.sum(jnp.where(neg_col == rrow, 1.0, 0.0), axis=0, keepdims=True) * (1.0 / nneg)
    live = lax.broadcasted_iota(jnp.int32, (cap, 1), 0).astype(f32) < count
    joined = two(head * ops)
    scores = mm3(joined, rhs_two, (1, 1))
    pos = jnp.sum(jnp.where(at_dst, scores, 0.0), axis=1, keepdims=True)
    coef = jax.nn.sigmoid(-pos)
    weight = times * (0.5 + 0.5 * jnp.tanh(0.5 * scores)) - jnp.where(at_dst, coef, 0.0)
    weight = two(jnp.where(live, weight, 0.0))
    g_joined = mm3(weight, rhs_two)
    rhs_grad = mm3(weight, joined, (0, 0))
    gh, gl = two(g_joined * ops)
    lhs_grad = mm(put_src, gl) + mm(put_src, gh)
    gh, gl = two(g_joined * head)
    rel_grad = mm(put_rel, gl) + mm(put_rel, gh)
    return lhs_grad, rhs_grad, rel_grad


def load_rel(rel_ref, pad_ref):
    pad_ref[384:, :] = jnp.zeros((128, nrel), f32)
    pad_ref[:width, :] = rel_ref[...]
    return two(pad_ref[...])


def store_rows(ref, pairs):
    for layer, rows in enumerate(pairs):
        for c in range(3):
            ref[pl.ds(layer * 3 + c, devices, stride=block_rows), :] = rows[:, c * 128 : (c + 1) * 128]
    ref[pl.ds(block_rows - 1, devices, stride=block_rows), :] = pairs[0][:, edge:] + pltpu.roll(pairs[1][:, edge:], 64, 1)


def store_half(ref, grad, which):
    begin = which * half
    store_rows(ref, (grad[begin : begin + devices, :], grad[begin + devices : begin + half, :]))


def first_kernel(own_ref, mate_ref, rel_ref, edge_ref, next_ref, grad_ref, grel_ref, head_ref, ops_ref, next_ops_ref, pad_ref):
    mine = load_part((own_ref, mate_ref))
    rel = load_rel(rel_ref, pad_ref)
    now, later = edge_ref[:edge_rows, :], edge_ref[edge_rows : 2 * edge_rows, :]
    lg, rg, relg = unit(mine[2], mine, heads(mine, now), operators(rel, now), now)
    grad_ref[...] = lg + rg
    grel_ref[...] = relg
    head_ref[...] = heads(mine, later)
    ops_ref[...] = operators(rel, later)
    next_ops_ref[...] = operators(rel, next_ref[...])


def second_kernel(
    own_ref, mate_ref, down_ref, down_mate_ref, up_ref, up_mate_ref, edge_ref, next_ref, grad_ref, grel_ref,
    head_ref, ops_ref, next_ops_ref,
    down_keep, down_give, up_keep, up_give, own_keep, own_give, rel_out,
):
    own_places = jnp.concatenate(main_and_tails(own_ref, block_rows, (0, 3), (0, 64))[3:] + main_and_tails(mate_ref, block_rows, (0, 3), (0, 64))[3:], axis=0)
    below = load_part((down_ref, down_mate_ref))
    above = load_part((up_ref, up_mate_ref))
    edges = next_ref[...]
    ug, dg, rel2 = unit(above[2], below, heads(above, edges), next_ops_ref[...], edges)
    store_half(up_keep, ug, 0)
    store_half(up_give, ug, 1)
    edges = edge_ref[edge_rows : 2 * edge_rows, :]
    lg, rg, rel1 = unit(own_places[:, tail : tail + 1], below, head_ref[...], ops_ref[...], edges)
    lg = lg + grad_ref[...]
    dg = dg + rg
    store_half(down_keep, dg, 0)
    store_half(down_give, dg, 1)
    store_half(own_keep, lg, 0)
    store_half(own_give, lg, 1)
    relg = grel_ref[...] + rel1 + rel2
    store_rows(rel_out, (relg[:devices, :], relg[devices:, :]))


def gather_kernel(keep_ref, give_ref, up_ref, down_ref, rel_ref, state_ref, rel_state_ref, out_ref, state_out, rel_state_out):
    for j in range(block_rows):
        rows = pl.ds(j, devices, stride=block_rows)
        sums = (keep_ref[rows, :] + give_ref[rows, :]) + (up_ref[rows, :] + down_ref[rows, :])
        rel = jnp.sum(rel_ref[rows, :], axis=0, keepdims=True)
        if j < block_rows - 1:
            out_ref[pl.ds(j, devices, stride=back_rows), :] = sums
            out_ref[pl.ds(block_rows - 1 + j, devices, stride=back_rows), :] = jnp.broadcast_to(rel, (devices, 128))
        else:
            both = sums + pltpu.roll(jnp.broadcast_to(rel, (devices, 128)), 32, 1)
            out_ref[pl.ds(back_rows - 1, devices, stride=back_rows), :] = both
    state_out[...] = state_ref[...]
    rel_state_out[...] = rel_state_ref[...]


def update(grads, value_ref, state_ref, new_value_ref, new_state_ref):
    state = state_ref[...] + sum(jnp.sum(g * g, axis=0, keepdims=True) for g in grads) * (1.0 / width)
    new_state_ref[...] = state
    scale = learn_rate / jnp.sqrt(state)
    for c in range(4):
        begin, end = c * 128, min((c + 1) * 128, width)
        new_value_ref[begin:end, :] = value_ref[begin:end, :] - scale * grads[c][: end - begin, :]


def finish_kernel(
    got_ref, perm_ref, emb_ref, state_ref, rel_ref, rel_state_ref, new_emb_ref, new_state_ref, new_rel_ref, new_rel_state_ref
):
    perm = perm_ref[...]
    grads = []
    for c, rows in enumerate(main_and_tails(got_ref, back_rows, (0, 3), (0, 64))):
        if c == 3:
            rows = jnp.where(lane_iota(rows.shape) < tail, rows, 0.0)
        high, mid, low = three(rows)
        grads.append(mm(high, perm, (0, 0)) + (mm(mid, perm, (0, 0)) + mm(low, perm, (0, 0))))
    update(grads, emb_ref, state_ref, new_emb_ref, new_state_ref)
    rel_grads = main_and_tails(got_ref, back_rows, (6, 9), (32, 96))
    rel_grads[3] = jnp.where(lane_iota(rel_grads[3].shape) < tail, rel_grads[3], 0.0)
    update([g.T for g in rel_grads], rel_ref, rel_state_ref, new_rel_ref, new_rel_state_ref)


def call(kernel, outs, mebibytes, scratch=(), flops=0, **options):
    return pl.pallas_call(
        kernel,
        out_shape=[jax.ShapeDtypeStruct(shape, dtype) for shape, dtype in outs],
        scratch_shapes=[pltpu.VMEM(shape, f32) if isinstance(shape, tuple) else shape for shape in scratch],
        compiler_params=pltpu.CompilerParams(vmem_limit_bytes=mebibytes << 20),
        cost_estimate=pl.CostEstimate(flops=flops, bytes_accessed=1 << 10, transcendentals=0),
        **options,
    )


def per_device(
    embedding,
    emb_state,
    entity_slot,
    relations,
    rel_state,
    edge_src,
    edge_rel,
    edge_dst,
    negatives,
    edge_count,
):
    flat = (devices * block_rows, 128)
    embedding, relations = embedding.T, relations.T
    given = (entity_slot.reshape(1, half), embedding, edge_src, edge_rel, edge_dst, negatives, edge_count.T)
    send, perm, edges = call(
        start_kernel,
        [(flat, f32), ((half, half), bf16), ((steps * edge_rows, 128), f32)],
        60,
        [pltpu.VMEM(a.shape, a.dtype) for a in given] + [(2 * 128, half), pltpu.SemaphoreType.DMA((7,))],
        in_specs=[pl.BlockSpec(memory_space=pltpu.HBM)] * 7,
    )(*given)
    own = exchanged(send)
    here = sent(edges[: 2 * edge_rows], edges_here)
    following = sent(edges[2 * edge_rows :], edges_next)
    own, here, following = lax.optimization_barrier((own, here, following))
    down = sent(own, go_up)
    up = sent(own, go_down)
    mate = sent(own, swap_cores)
    square = ((part, wide), f32)
    grad, grel, head, ops, next_ops = call(
        first_kernel, [square, ((nrel, wide), f32), square, square, square], 24, [(wide, nrel)]
    )(own, mate, relations, here, following)
    down, up, grad, grel = lax.optimization_barrier((down, up, grad, grel))
    down_mate = sent(down, swap_cores)
    up_mate = sent(up, swap_cores)
    down_keep, down_give, up_keep, up_give, own_keep, own_give, rel_part = call(second_kernel, [(flat, f32)] * 7, 32)(
        own, mate, down, down_mate, up, up_mate, here, following, grad, grel, head, ops, next_ops
    )
    down_sum = down_keep + sent(down_give, swap_cores)
    up_sum = up_keep + sent(up_give, swap_cores)
    own_got = sent(own_give, swap_cores)
    from_up = sent(down_sum, go_down)
    from_down = sent(up_sum, go_up)
    rel_got = exchanged(rel_part)
    row = ((1, half), f32)
    back, state, rel_state = call(gather_kernel, [((devices * back_rows, 128), f32), row, row], 16)(
        own_keep, own_got, from_up, from_down, rel_got, emb_state.reshape(1, half), rel_state.reshape(1, nrel)
    )
    new_embedding, new_state, new_relations, new_rel_state = call(
        finish_kernel, [((width, half), f32), row, ((width, nrel), f32), row], 16
    )(exchanged(back), perm, embedding, state, relations, rel_state)
    return (
        new_embedding.T,
        new_state.reshape(half),
        new_relations.T,
        new_rel_state.reshape(nrel),
    )


def solution(mesh):
    placed = (
        P(axes, None),
        P(axes),
        P(axes),
        P(),
        P(),
        P(None, axes),
        P(None, axes),
        P(None, axes),
        P(None, axes),
        P(None, axes),
    )
    return jax.shard_map(
        per_device,
        mesh=mesh,
        in_specs=placed,
        out_specs=(P(axes, None), P(axes), P(), P()),
        check_vma=False,
    )
```

```python
import jax
import jax.numpy as jnp
from jax import lax
from jax.experimental import pallas as pl
from jax.experimental.pallas import tpu as pltpu
from jax.sharding import PartitionSpec as P

learn_rate = 0.1
axes = ("blk", "rows")
devices = 128
chips = 64
part = 512
half = 256
width = 400
wide = 512
nrel = 256
cap = 512
nneg = 1000
steps = 3
edge_rows = 24
edge = 384
tail = width - edge
ent_rows = 13
rel_rows = 7
back_rows = 19
ent_lanes = (0, 32, 64, 96)
f32 = jnp.float32
bf16 = jnp.bfloat16


def device_at(place, core):
    visit, y, step = place // 32, place // 8 % 4, place % 8
    x = step if step < 4 else 7 - step
    odd = (y % 2) if step < 4 else 1 - y % 2
    z = 2 * visit + odd if y < 3 or odd else (2 * visit + 2) % 4
    block = (((z % 2) * 4 + y) * 4 + x) * 2 + core
    return block * 2 + z // 2


def every(source, target):
    return [(source(p, h), target(p, h)) for p in range(chips) for h in range(2)]


swap_cores = every(device_at, lambda p, h: device_at(p, 1 - h))
go_up = every(device_at, lambda p, h: device_at((p + 1) % chips, h))
go_down = every(device_at, lambda p, h: device_at((p - 1) % chips, h))
edges_next = every(lambda p, h: 2 * ((p + 1) % chips) + h, device_at)
same_core = [[device_at(p, h) for p in range(chips)] for h in range(2)]
edges_here = every(lambda p, h: 2 * p + h, device_at)


def sent(value, pairs):
    return lax.ppermute(value, axes, pairs)


def exchanged(value):
    rows = value.shape[0]
    blocks = value.reshape(chips, rows // chips, 1, 128)
    got = lax.all_to_all(blocks, axes, split_axis=0, concat_axis=0, axis_index_groups=same_core, tiled=True)
    return got.reshape(rows, 128)


def two(value):
    high = value.astype(bf16)
    return high, (value - high.astype(f32)).astype(bf16)


def three(value):
    high = value.astype(bf16)
    rest = value - high.astype(f32)
    mid = rest.astype(bf16)
    return high, mid, (rest - mid.astype(f32)).astype(bf16)


def mm(a, b, contract=(1, 0)):
    return lax.dot_general(
        a, b, (((contract[0],), (contract[1],)), ((), ())), preferred_element_type=f32
    )


def mm3(a, b, contract=(1, 0)):
    return (mm(a[0], b[1], contract) + mm(a[1], b[0], contract)) + mm(a[0], b[0], contract)


def lane_iota(shape):
    return lax.broadcasted_iota(jnp.int32, shape, len(shape) - 1)


def start_kernel(*refs):
    far, (send_ref, perm_ref, edge_ref), near = refs[:7], refs[7:10], refs[10:17]
    last_ref, arrived = refs[17:]
    copies = [pltpu.make_async_copy(a, b, arrived.at[i]) for i, (a, b) in enumerate(zip(far, near))]
    for copy in copies:
        copy.start()
    slot_ref, emb_ref, src_ref, rel_ref, dst_ref, neg_ref, count_ref = near
    copies[0].wait()
    slot = slot_ref[...]
    match = lax.broadcasted_iota(jnp.int32, (chips, half), 0) == slot // part
    before = (
        lax.broadcasted_iota(jnp.int32, (half, half), 0) < lane_iota((half, half))
    ).astype(f32).astype(bf16)
    earlier = mm(match.astype(f32).astype(bf16), before)
    picks = [jnp.where(match, jnp.where(jnp.abs(earlier - layer) < 0.5, 1.0, 0.0), 0.0) for layer in range(4)]
    perm = jnp.concatenate(picks, axis=0).astype(bf16)
    perm_ref[...] = perm
    last_ref[...] = jnp.zeros(last_ref.shape, f32)
    copies[1].wait()
    last_ref[:tail, :] = emb_ref[edge:, :]
    last_ref[tail : tail + 1, :] = (slot & (part - 1)).astype(f32)
    outs = []
    for c in range(4):
        high, mid, low = three(emb_ref[c * 128 : (c + 1) * 128, :] if c < 3 else last_ref[...])
        outs.append(mm(perm, high, (1, 1)) + (mm(perm, mid, (1, 1)) + mm(perm, low, (1, 1))))
    store_rows(send_ref, outs, 0, 4)
    for copy in copies[2:]:
        copy.wait()
    for s in range(steps):
        base = s * edge_rows
        for j in range(4):
            lanes = slice(j * 128, (j + 1) * 128)
            edge_ref[base + j : base + j + 1, :] = src_ref[s : s + 1, lanes].astype(f32)
            edge_ref[base + 4 + j : base + 5 + j, :] = rel_ref[s : s + 1, lanes].astype(f32)
            edge_ref[base + 8 + j : base + 9 + j, :] = dst_ref[s : s + 1, lanes].astype(f32)
        edge_ref[base + 19 : base + 20, :] = jnp.full((1, 128), -1.0, f32)
        for j in range(8):
            end = min((j + 1) * 128, nneg)
            edge_ref[base + 12 + j : base + 13 + j, : end - j * 128] = neg_ref[
                s : s + 1, j * 128 : end
            ].astype(f32)
        edge_ref[base + 20 : base + edge_rows, :] = jnp.broadcast_to(
            count_ref[:, s : s + 1].astype(f32), (edge_rows - 20, 128)
        )


def rolled(value, lanes):
    return pltpu.roll(value, lanes, 1) if lanes % 128 else value


def main_and_tails(ref, rows, firsts, lanes):
    blocks = []
    for c in range(3):
        blocks.append(jnp.concatenate([ref[pl.ds(first + c, chips, stride=rows), :] for first in firsts], axis=0))
    last = ref[pl.ds(rows - 1, chips, stride=rows), :]
    return blocks + [jnp.concatenate([rolled(last, (128 - lane) % 128) for lane in lanes], axis=0)]


def ent_blocks(ref, rows):
    return main_and_tails(ref, rows, (0, 3, 6, 9), ent_lanes)


def store_rows(ref, columns, begin, layers):
    rows = 3 * layers + 1
    tails = 0.0
    for layer in range(layers):
        now = slice(begin + layer * chips, begin + (layer + 1) * chips)
        for c in range(3):
            ref[pl.ds(layer * 3 + c, chips, stride=rows), :] = columns[c][now, :]
        tails = tails + rolled(columns[3][now, :], ent_lanes[layer])
    ref[pl.ds(rows - 1, chips, stride=rows), :] = tails


def column_blocks(value):
    return [value[:, c * 128 : (c + 1) * 128] for c in range(4)]


def load_part(refs):
    halves = [ent_blocks(ref, ent_rows) for ref in refs]
    blocks = [jnp.concatenate(pair, axis=0) for pair in zip(*halves)]
    last = blocks[3]
    column = last[:, tail : tail + 1]
    row = last.T[tail : tail + 1, :]
    blocks[3] = jnp.where(lane_iota(last.shape) < tail, last, 0.0)
    full = jnp.concatenate(blocks, axis=1)
    return two(full), row, column


def onehot(a, b):
    return jnp.where(a == b, 1.0, 0.0).astype(bf16)


def edge_views(edges):
    flipped = edges.T
    row = lambda first: jnp.concatenate([edges[first + j : first + j + 1, :] for j in range(4)], axis=1)
    column = lambda first, n: jnp.concatenate([flipped[:, first + j : first + j + 1] for j in range(n)], axis=0)
    return row, column


def heads(lhs, edges):
    (high, low), row, _ = lhs
    pick = onehot(edge_views(edges)[1](0, 4), row)
    return mm(pick, low) + mm(pick, high)


def operators(rel, edges):
    high, low = rel
    pick = onehot(edge_views(edges)[1](4, 4), lane_iota((cap, nrel)).astype(f32))
    return mm(pick, low, (1, 1)) + mm(pick, high, (1, 1))


def unit(lcol, rhs, head, ops, edges, core):
    rhs_two, rrow, _ = rhs
    row, column = edge_views(edges)
    dst_col, neg_col = column(8, 4), column(12, 8)
    count = edges[20:21, 0:1]
    put_src = onehot(lcol, row(0))
    row_ids = lax.broadcasted_iota(jnp.int32, (nrel, 1), 0).astype(f32)
    row_ids = jnp.where(core > 0.5, jnp.where(row_ids < nrel // 2, row_ids + nrel // 2, row_ids - nrel // 2), row_ids)
    put_rel = onehot(row_ids, row(4))
    at_dst = dst_col == rrow
    times = jnp.sum(jnp.where(neg_col == rrow, 1.0, 0.0), axis=0, keepdims=True) * (1.0 / nneg)
    live = lax.broadcasted_iota(jnp.int32, (cap, 1), 0).astype(f32) < count
    joined = two(head * ops)
    scores = mm3(joined, rhs_two, (1, 1))
    pos = jnp.sum(jnp.where(at_dst, scores, 0.0), axis=1, keepdims=True)
    coef = jax.nn.sigmoid(-pos)
    weight = times * (0.5 + 0.5 * jnp.tanh(0.5 * scores)) - jnp.where(at_dst, coef, 0.0)
    weight = two(jnp.where(live, weight, 0.0))
    g_joined = mm3(weight, rhs_two)
    rhs_grad = mm3(weight, joined, (0, 0))
    gh, gl = two(g_joined * ops)
    lhs_grad = mm(put_src, gl) + mm(put_src, gh)
    gh, gl = two(g_joined * head)
    rel_grad = mm(put_rel, gl) + mm(put_rel, gh)
    return lhs_grad, rhs_grad, rel_grad


def load_rel(rel_ref, pad_ref):
    pad_ref[384:, :] = jnp.zeros((128, nrel), f32)
    pad_ref[:width, :] = rel_ref[...]
    return two(pad_ref[...])


def store_half(ref, grad, which):
    store_rows(ref, column_blocks(grad), which * half, 4)


def first_kernel(
    own_ref, mate_ref, rel_ref, edge_ref, next_ref, core_ref, state_ref, rel_state_ref,
    grad_ref, grel_ref, head_ref, ops_ref, next_ops_ref, state_out, rel_state_out, pad_ref,
):
    mine = load_part((own_ref, mate_ref))
    rel = load_rel(rel_ref, pad_ref)
    now, later = edge_ref[:edge_rows, :], edge_ref[edge_rows : 2 * edge_rows, :]
    lg, rg, relg = unit(mine[2], mine, heads(mine, now), operators(rel, now), now, core_ref[...])
    grad_ref[...] = lg + rg
    grel_ref[...] = relg
    head_ref[...] = heads(mine, later)
    ops_ref[...] = operators(rel, later)
    next_ops_ref[...] = operators(rel, next_ref[...])
    state_out[...] = state_ref[...]
    rel_state_out[...] = rel_state_ref[...]


def second_kernel(
    own_ref, mate_ref, down_ref, down_mate_ref, up_ref, up_mate_ref, edge_ref, next_ref, grad_ref, grel_ref,
    head_ref, ops_ref, next_ops_ref, core_ref,
    down_keep, down_give, up_keep, up_give, own_keep, own_give, rel_keep, rel_give,
):
    own_places = jnp.concatenate([ent_blocks(ref, ent_rows)[3] for ref in (own_ref, mate_ref)], axis=0)
    below = load_part((down_ref, down_mate_ref))
    above = load_part((up_ref, up_mate_ref))
    edges = next_ref[...]
    ug, dg, rel2 = unit(above[2], below, heads(above, edges), next_ops_ref[...], edges, core_ref[...])
    store_half(up_keep, ug, 0)
    store_half(up_give, ug, 1)
    edges = edge_ref[edge_rows : 2 * edge_rows, :]
    lg, rg, rel1 = unit(own_places[:, tail : tail + 1], below, head_ref[...], ops_ref[...], edges, core_ref[...])
    lg = lg + grad_ref[...]
    dg = dg + rg
    store_half(down_keep, dg, 0)
    store_half(down_give, dg, 1)
    store_half(own_keep, lg, 0)
    store_half(own_give, lg, 1)
    relg = grel_ref[...] + rel1 + rel2
    store_rows(rel_keep, column_blocks(relg), 0, 2)
    store_rows(rel_give, column_blocks(relg), nrel // 2, 2)


def gather_kernel(keep_ref, give_ref, up_ref, down_ref, rel_ref, out_ref):
    for j in range(ent_rows):
        rows = pl.ds(j, chips, stride=ent_rows)
        sums = (keep_ref[rows, :] + give_ref[rows, :]) + (up_ref[rows, :] + down_ref[rows, :])
        if j < ent_rows - 1:
            out_ref[pl.ds(j, chips, stride=back_rows), :] = sums
    for j in range(rel_rows):
        rel = jnp.sum(rel_ref[pl.ds(j, chips, stride=rel_rows), :], axis=0, keepdims=True)
        rel = jnp.broadcast_to(rel, (chips, 128))
        if j < rel_rows - 1:
            out_ref[pl.ds(ent_rows - 1 + j, chips, stride=back_rows), :] = rel
        else:
            out_ref[pl.ds(back_rows - 1, chips, stride=back_rows), :] = sums + rolled(rel, tail)


def update(grads, value_ref, state_ref, new_value_ref, new_state_ref):
    state = state_ref[...] + sum(jnp.sum(g * g, axis=0, keepdims=True) for g in grads) * (1.0 / width)
    new_state_ref[...] = state
    scale = learn_rate / jnp.sqrt(state)
    for c in range(4):
        begin, end = c * 128, min((c + 1) * 128, width)
        new_value_ref[begin:end, :] = value_ref[begin:end, :] - scale * grads[c][: end - begin, :]


def rel_half_kernel(got_ref, out_ref):
    blocks = main_and_tails(got_ref, back_rows, (12, 15), (tail, 32 + tail))
    for c in range(4):
        rows = blocks[c] if c < 3 else jnp.where(lane_iota(blocks[c].shape) < tail, blocks[c], 0.0)
        out_ref[c * 128 : (c + 1) * 128, :] = rows


def entity_kernel(got_ref, perm_ref, emb_ref, state_ref, new_emb_ref, new_state_ref):
    perm = perm_ref[...]
    grads = []
    for c, rows in enumerate(ent_blocks(got_ref, back_rows)):
        if c == 3:
            rows = jnp.where(lane_iota(rows.shape) < tail, rows, 0.0)
        high, mid, low = three(rows)
        grads.append(mm(high, perm, (0, 0)) + (mm(mid, perm, (0, 0)) + mm(low, perm, (0, 0))))
    update(grads, emb_ref, state_ref, new_emb_ref, new_state_ref)


def relation_kernel(own_ref, mate_ref, core_ref, rel_ref, rel_state_ref, new_rel_ref, new_rel_state_ref):
    first = core_ref[...] < 0.5
    grads = []
    for c in range(4):
        own, mate = own_ref[c * 128 : (c + 1) * 128, :].T, mate_ref[c * 128 : (c + 1) * 128, :].T
        grads.append(jnp.concatenate([jnp.where(first, own, mate), jnp.where(first, mate, own)], axis=1))
    update(grads, rel_ref, rel_state_ref, new_rel_ref, new_rel_state_ref)


def call(kernel, outs, mebibytes, scratch=(), flops=0, **options):
    return pl.pallas_call(
        kernel,
        out_shape=[jax.ShapeDtypeStruct(shape, dtype) for shape, dtype in outs],
        scratch_shapes=[pltpu.VMEM(shape, f32) if isinstance(shape, tuple) else shape for shape in scratch],
        compiler_params=pltpu.CompilerParams(vmem_limit_bytes=mebibytes << 20),
        cost_estimate=pl.CostEstimate(flops=flops, bytes_accessed=1 << 10, transcendentals=0),
        **options,
    )


def per_device(
    embedding,
    emb_state,
    entity_slot,
    relations,
    rel_state,
    edge_src,
    edge_rel,
    edge_dst,
    negatives,
    edge_count,
):
    flat = (chips * ent_rows, 128)
    core = (lax.axis_index("blk") % 2).astype(f32).reshape(1, 1)
    embedding, relations = embedding.T, relations.T
    given = (entity_slot.reshape(1, half), embedding, edge_src, edge_rel, edge_dst, negatives, edge_count.T)
    send, perm, edges = call(
        start_kernel,
        [(flat, f32), ((half, half), bf16), ((steps * edge_rows, 128), f32)],
        60,
        [pltpu.VMEM(a.shape, a.dtype) for a in given] + [(128, half), pltpu.SemaphoreType.DMA((7,))],
        in_specs=[pl.BlockSpec(memory_space=pltpu.HBM)] * 7,
    )(*given)
    own = exchanged(send)
    here = sent(edges[: 2 * edge_rows], edges_here)
    following = sent(edges[2 * edge_rows :], edges_next)
    own, here, following = lax.optimization_barrier((own, here, following))
    down = sent(own, go_up)
    up = sent(own, go_down)
    mate = sent(own, swap_cores)
    square, row = ((part, wide), f32), ((1, half), f32)
    grad, grel, head, ops, next_ops, state, rel_state = call(
        first_kernel, [square, ((nrel, wide), f32), square, square, square, row, row], 24, [(wide, nrel)]
    )(own, mate, relations, here, following, core, emb_state.reshape(1, half), rel_state.reshape(1, nrel))
    down, up, grad, grel = lax.optimization_barrier((down, up, grad, grel))
    down_mate = sent(down, swap_cores)
    up_mate = sent(up, swap_cores)
    rel_flat = ((chips * rel_rows, 128), f32)
    down_keep, down_give, up_keep, up_give, own_keep, own_give, rel_keep, rel_give = call(
        second_kernel, [(flat, f32)] * 6 + [rel_flat] * 2, 32
    )(own, mate, down, down_mate, up, up_mate, here, following, grad, grel, head, ops, next_ops, core)
    rel_sum = rel_keep + sent(rel_give, swap_cores)
    down_sum = down_keep + sent(down_give, swap_cores)
    up_sum = up_keep + sent(up_give, swap_cores)
    own_got = sent(own_give, swap_cores)
    from_up = sent(down_sum, go_down)
    from_down = sent(up_sum, go_up)
    rel_got = exchanged(rel_sum)
    (back,) = call(gather_kernel, [((chips * back_rows, 128), f32)], 16)(own_keep, own_got, from_up, from_down, rel_got)
    got = exchanged(back)
    (rel_own,) = call(rel_half_kernel, [((wide, 128), f32)], 8)(got)
    rel_mate = sent(rel_own, swap_cores)
    new_embedding, new_state = call(entity_kernel, [((width, half), f32), row], 16)(got, perm, embedding, state)
    new_relations, new_rel_state = call(relation_kernel, [((width, nrel), f32), row], 8)(
        rel_own, rel_mate, core, relations, rel_state
    )
    return (
        new_embedding.T,
        new_state.reshape(half),
        new_relations.T,
        new_rel_state.reshape(nrel),
    )


def solution(mesh):
    placed = (
        P(axes, None),
        P(axes),
        P(axes),
        P(),
        P(),
        P(None, axes),
        P(None, axes),
        P(None, axes),
        P(None, axes),
        P(None, axes),
    )
    return jax.shard_map(
        per_device,
        mesh=mesh,
        in_specs=placed,
        out_specs=(P(axes, None), P(axes), P(), P()),
        check_vma=False,
    )
```

```python
import jax
import jax.numpy as jnp
from jax import lax
from jax.experimental import pallas as pl
from jax.experimental.pallas import tpu as pltpu
from jax.sharding import PartitionSpec as P

learn_rate = 0.1
axes = ("blk", "rows")
devices = 128
chips = 64
part = 512
half = 256
width = 400
wide = 512
nrel = 256
cap = 512
nneg = 1000
steps = 3
edge_rows = 24
edge = 384
tail = width - edge
out_rows = 39
ent_rows = 13
rel_rows = 7
back_rows = 19
ent_lanes = (0, 32, 64, 96)
f32 = jnp.float32
bf16 = jnp.bfloat16


def device_at(place, core):
    visit, y, step = place // 32, place // 8 % 4, place % 8
    x = step if step < 4 else 7 - step
    odd = (y % 2) if step < 4 else 1 - y % 2
    z = 2 * visit + odd if y < 3 or odd else (2 * visit + 2) % 4
    block = (((z % 2) * 4 + y) * 4 + x) * 2 + core
    return block * 2 + z // 2


def every(source, target):
    return [(source(p, h), target(p, h)) for p in range(chips) for h in range(2)]


swap_cores = every(device_at, lambda p, h: device_at(p, 1 - h))
go_up = every(device_at, lambda p, h: device_at((p + 1) % chips, h))
go_down = every(device_at, lambda p, h: device_at((p - 1) % chips, h))
edges_next = every(lambda p, h: 2 * ((p + 1) % chips) + h, device_at)
same_core = [[device_at(p, h) for p in range(chips)] for h in range(2)]
edges_here = every(lambda p, h: 2 * p + h, device_at)


def sent(value, pairs):
    return lax.ppermute(value, axes, pairs)


def exchanged(value):
    rows = value.shape[0]
    blocks = value.reshape(chips, rows // chips, 1, 128)
    got = lax.all_to_all(blocks, axes, split_axis=0, concat_axis=0, axis_index_groups=same_core, tiled=True)
    return got.reshape(rows, 128)


def two(value):
    high = value.astype(bf16)
    return high, (value - high.astype(f32)).astype(bf16)


def three(value):
    high = value.astype(bf16)
    rest = value - high.astype(f32)
    mid = rest.astype(bf16)
    return high, mid, (rest - mid.astype(f32)).astype(bf16)


def mm(a, b, contract=(1, 0)):
    return lax.dot_general(
        a, b, (((contract[0],), (contract[1],)), ((), ())), preferred_element_type=f32
    )


def mm3(a, b, contract=(1, 0)):
    return (mm(a[0], b[1], contract) + mm(a[1], b[0], contract)) + mm(a[0], b[0], contract)


def lane_iota(shape):
    return lax.broadcasted_iota(jnp.int32, shape, len(shape) - 1)


def start_kernel(*refs):
    far, (send_ref, perm_ref, edge_ref), near = refs[:7], refs[7:10], refs[10:17]
    last_ref, arrived = refs[17:]
    copies = [pltpu.make_async_copy(a, b, arrived.at[i]) for i, (a, b) in enumerate(zip(far, near))]
    for copy in copies:
        copy.start()
    slot_ref, emb_ref, src_ref, rel_ref, dst_ref, neg_ref, count_ref = near
    copies[0].wait()
    slot = slot_ref[...]
    match = lax.broadcasted_iota(jnp.int32, (chips, half), 0) == slot // part
    before = (
        lax.broadcasted_iota(jnp.int32, (half, half), 0) < lane_iota((half, half))
    ).astype(f32).astype(bf16)
    earlier = mm(match.astype(f32).astype(bf16), before)
    picks = [jnp.where(match, jnp.where(jnp.abs(earlier - layer) < 0.5, 1.0, 0.0), 0.0) for layer in range(4)]
    perm = jnp.concatenate(picks, axis=0).astype(bf16)
    perm_ref[...] = perm
    last_ref[...] = jnp.zeros(last_ref.shape, f32)
    copies[1].wait()
    last_ref[:tail, :] = emb_ref[edge:, :]
    last_ref[tail : tail + 1, :] = (slot & (part - 1)).astype(f32)
    outs = []
    for c in range(4):
        high, mid, low = three(emb_ref[c * 128 : (c + 1) * 128, :] if c < 3 else last_ref[...])
        outs.append(mm(perm, high, (1, 1)) + (mm(perm, mid, (1, 1)) + mm(perm, low, (1, 1))))
    for which, shift in enumerate((0, 1, chips - 1)):
        store_rows(send_ref, outs, 0, 4, out_rows, which * ent_rows, shift)
    for copy in copies[2:]:
        copy.wait()
    for s in range(steps):
        base = s * edge_rows
        for j in range(4):
            lanes = slice(j * 128, (j + 1) * 128)
            edge_ref[base + j : base + j + 1, :] = src_ref[s : s + 1, lanes].astype(f32)
            edge_ref[base + 4 + j : base + 5 + j, :] = rel_ref[s : s + 1, lanes].astype(f32)
            edge_ref[base + 8 + j : base + 9 + j, :] = dst_ref[s : s + 1, lanes].astype(f32)
        edge_ref[base + 19 : base + 20, :] = jnp.full((1, 128), -1.0, f32)
        for j in range(8):
            end = min((j + 1) * 128, nneg)
            edge_ref[base + 12 + j : base + 13 + j, : end - j * 128] = neg_ref[
                s : s + 1, j * 128 : end
            ].astype(f32)
        edge_ref[base + 20 : base + edge_rows, :] = jnp.broadcast_to(
            count_ref[:, s : s + 1].astype(f32), (edge_rows - 20, 128)
        )


def rolled(value, lanes):
    return pltpu.roll(value, lanes, 1) if lanes % 128 else value


def main_and_tails(ref, rows, firsts, lanes, last_row):
    blocks = []
    for c in range(3):
        blocks.append(jnp.concatenate([ref[pl.ds(first + c, chips, stride=rows), :] for first in firsts], axis=0))
    last = ref[pl.ds(last_row, chips, stride=rows), :]
    return blocks + [jnp.concatenate([rolled(last, (128 - lane) % 128) for lane in lanes], axis=0)]


def ent_blocks(ref, rows, base, last_row):
    return main_and_tails(ref, rows, [base + 3 * layer for layer in range(4)], ent_lanes, last_row)


def store_rows(ref, columns, begin, layers, rows=None, base=0, shift=0):
    rows = rows or 3 * layers + 1
    turned = lambda value: pltpu.roll(value, shift, 0) if shift else value
    tails = 0.0
    for layer in range(layers):
        now = slice(begin + layer * chips, begin + (layer + 1) * chips)
        for c in range(3):
            ref[pl.ds(base + layer * 3 + c, chips, stride=rows), :] = turned(columns[c][now, :])
        tails = tails + rolled(columns[3][now, :], ent_lanes[layer])
    ref[pl.ds(base + 3 * layers, chips, stride=rows), :] = turned(tails)


def column_blocks(value):
    return [value[:, c * 128 : (c + 1) * 128] for c in range(4)]


def load_part(refs, which):
    base = which * ent_rows
    halves = [ent_blocks(ref, out_rows, base, base + ent_rows - 1) for ref in refs]
    blocks = [jnp.concatenate(pair, axis=0) for pair in zip(*halves)]
    last = blocks[3]
    column = last[:, tail : tail + 1]
    row = last.T[tail : tail + 1, :]
    blocks[3] = jnp.where(lane_iota(last.shape) < tail, last, 0.0)
    full = jnp.concatenate(blocks, axis=1)
    return two(full), row, column


def onehot(a, b):
    return jnp.where(a == b, 1.0, 0.0).astype(bf16)


def edge_views(edges):
    flipped = edges.T
    row = lambda first: jnp.concatenate([edges[first + j : first + j + 1, :] for j in range(4)], axis=1)
    column = lambda first, n: jnp.concatenate([flipped[:, first + j : first + j + 1] for j in range(n)], axis=0)
    return row, column


def heads(lhs, edges):
    (high, low), row, _ = lhs
    pick = onehot(edge_views(edges)[1](0, 4), row)
    return mm(pick, low) + mm(pick, high)


def operators(rel, edges):
    high, low = rel
    pick = onehot(edge_views(edges)[1](4, 4), lane_iota((cap, nrel)).astype(f32))
    return mm(pick, low, (1, 1)) + mm(pick, high, (1, 1))


def terms(rhs, head, ops, edge_sets, core):
    rhs_two, rrow, _ = rhs
    row_ids = lax.broadcasted_iota(jnp.int32, (nrel, 1), 0).astype(f32)
    row_ids = jnp.where(core > 0.5, jnp.where(row_ids < nrel // 2, row_ids + nrel // 2, row_ids - nrel // 2), row_ids)
    joined = two(head * ops)
    scores = mm3(joined, rhs_two, (1, 1))
    weights, put_rels = [], []
    for i, edges in enumerate(edge_sets):
        row, column = edge_views(edges)
        at_dst = column(8, 4) == rrow
        times = jnp.sum(jnp.where(column(12, 8) == rrow, 1.0, 0.0), axis=0, keepdims=True) * (1.0 / nneg)
        live = lax.broadcasted_iota(jnp.int32, (cap, 1), 0).astype(f32) < edges[20:21, 0:1]
        score = scores[i * cap : (i + 1) * cap, :]
        pos = jnp.sum(jnp.where(at_dst, score, 0.0), axis=1, keepdims=True)
        weight = times * (0.5 + 0.5 * jnp.tanh(0.5 * score)) - jnp.where(at_dst, jax.nn.sigmoid(-pos), 0.0)
        weights.append(jnp.where(live, weight, 0.0))
        put_rels.append(onehot(row_ids, row(4)))
    weight = two(jnp.concatenate(weights, axis=0))
    g_joined = mm3(weight, rhs_two)
    gh, gl = two(g_joined * head)
    put_rel = jnp.concatenate(put_rels, axis=1)
    rel_grad = mm(put_rel, gl) + mm(put_rel, gh)
    return weight, joined, two(g_joined * ops), rel_grad


def put_back(lcol, edges, grads):
    put_src = onehot(lcol, edge_views(edges)[0](0))
    return mm(put_src, grads[1]) + mm(put_src, grads[0])


def load_rel(rel_ref, pad_ref):
    pad_ref[384:, :] = jnp.zeros((128, nrel), f32)
    pad_ref[:width, :] = rel_ref[...]
    return two(pad_ref[...])


def store_half(ref, grad, which):
    store_rows(ref, column_blocks(grad), which * half, 4)


def operator_kernel(rel_ref, edge_ref, next_ref, state_ref, rel_state_ref, ops_ref, state_out, rel_state_out, pad_ref):
    rel = load_rel(rel_ref, pad_ref)
    sets = (edge_ref[:edge_rows, :], edge_ref[edge_rows : 2 * edge_rows, :], next_ref[...])
    for i, edges in enumerate(sets):
        ops_ref[i * cap : (i + 1) * cap, :] = operators(rel, edges)
    state_out[...] = state_ref[...]
    rel_state_out[...] = rel_state_ref[...]


def unit_kernel(
    own_ref, mate_ref, ops_ref, edge_ref, next_ref, core_ref,
    down_keep, down_give, up_keep, up_give, rel_keep, rel_give, weight_ref, joined_ref, head_grad_ref, place_ref,
):
    mine, below, above = [load_part((own_ref, mate_ref), which) for which in range(3)]
    core = core_ref[...]
    first, now, later = edge_ref[:edge_rows, :], edge_ref[edge_rows : 2 * edge_rows, :], next_ref[...]
    weight, joined, grads, rel0 = terms(mine, heads(mine, first), ops_ref[:cap, :], [first], core)
    for i in range(2):
        weight_ref[i * cap : (i + 1) * cap, :] = weight[i]
        joined_ref[i * cap : (i + 1) * cap, :] = joined[i]
        head_grad_ref[i * cap : (i + 1) * cap, :] = grads[i]
    head = jnp.concatenate([heads(mine, now), heads(above, later)], axis=0)
    weight, joined, grads, relg = terms(below, head, ops_ref[cap:, :], [now, later], core)
    for i in range(2):
        head_grad_ref[(i + 2) * cap : (i + 3) * cap, :] = grads[i][:cap, :]
    place_ref[...] = jnp.broadcast_to(mine[2], (part, 128))
    dg = mm3(weight, joined, (0, 0))
    ug = put_back(above[2], later, (grads[0][cap:, :], grads[1][cap:, :]))
    relg = relg + rel0
    store_half(up_keep, ug, 0)
    store_half(up_give, ug, 1)
    store_half(down_keep, dg, 0)
    store_half(down_give, dg, 1)
    store_rows(rel_keep, column_blocks(relg), 0, 2)
    store_rows(rel_give, column_blocks(relg), nrel // 2, 2)


def own_kernel(weight_ref, joined_ref, head_grad_ref, place_ref, edge_ref, own_keep, own_give):
    pair = lambda ref, i: (ref[i * cap : (i + 1) * cap, :], ref[(i + 1) * cap : (i + 2) * cap, :])
    places = place_ref[:, 0:1]
    lg = mm3(pair(weight_ref, 0), pair(joined_ref, 0), (0, 0))
    lg = lg + put_back(places, edge_ref[:edge_rows, :], pair(head_grad_ref, 0))
    lg = lg + put_back(places, edge_ref[edge_rows : 2 * edge_rows, :], pair(head_grad_ref, 2))
    store_half(own_keep, lg, 0)
    store_half(own_give, lg, 1)


def add_kernel(*refs):
    for a, b, out in zip(refs[:3], refs[3:6], refs[6:]):
        out[...] = a[...] + b[...]


def gather_kernel(keep_ref, give_ref, up_ref, down_ref, rel_ref, out_ref):
    for j in range(ent_rows):
        rows = pl.ds(j, chips, stride=ent_rows)
        sums = (keep_ref[rows, :] + give_ref[rows, :]) + (up_ref[rows, :] + down_ref[rows, :])
        if j < ent_rows - 1:
            out_ref[pl.ds(j, chips, stride=back_rows), :] = sums
    for j in range(rel_rows):
        rel = jnp.sum(rel_ref[pl.ds(j, chips, stride=rel_rows), :], axis=0, keepdims=True)
        rel = jnp.broadcast_to(rel, (chips, 128))
        if j < rel_rows - 1:
            out_ref[pl.ds(ent_rows - 1 + j, chips, stride=back_rows), :] = rel
        else:
            out_ref[pl.ds(back_rows - 1, chips, stride=back_rows), :] = sums + rolled(rel, tail)


def update(grads, value_ref, state_ref, new_value_ref, new_state_ref):
    state = state_ref[...] + sum(jnp.sum(g * g, axis=0, keepdims=True) for g in grads) * (1.0 / width)
    new_state_ref[...] = state
    scale = learn_rate / jnp.sqrt(state)
    for c in range(4):
        begin, end = c * 128, min((c + 1) * 128, width)
        new_value_ref[begin:end, :] = value_ref[begin:end, :] - scale * grads[c][: end - begin, :]


def rel_half_kernel(got_ref, out_ref):
    blocks = main_and_tails(got_ref, back_rows, (12, 15), (tail, 32 + tail), back_rows - 1)
    for c in range(4):
        rows = blocks[c] if c < 3 else jnp.where(lane_iota(blocks[c].shape) < tail, blocks[c], 0.0)
        out_ref[c * 128 : (c + 1) * 128, :] = rows


def entity_kernel(got_ref, perm_ref, emb_ref, state_ref, new_emb_ref, new_state_ref):
    perm = perm_ref[...]
    grads = []
    for c, rows in enumerate(ent_blocks(got_ref, back_rows, 0, back_rows - 1)):
        if c == 3:
            rows = jnp.where(lane_iota(rows.shape) < tail, rows, 0.0)
        high, mid, low = three(rows)
        grads.append(mm(high, perm, (0, 0)) + (mm(mid, perm, (0, 0)) + mm(low, perm, (0, 0))))
    update(grads, emb_ref, state_ref, new_emb_ref, new_state_ref)


def relation_kernel(own_ref, mate_ref, core_ref, rel_ref, rel_state_ref, new_rel_ref, new_rel_state_ref):
    first = core_ref[...] < 0.5
    grads = []
    for c in range(4):
        own, mate = own_ref[c * 128 : (c + 1) * 128, :].T, mate_ref[c * 128 : (c + 1) * 128, :].T
        grads.append(jnp.concatenate([jnp.where(first, own, mate), jnp.where(first, mate, own)], axis=1))
    update(grads, rel_ref, rel_state_ref, new_rel_ref, new_rel_state_ref)


def call(kernel, outs, mebibytes, scratch=(), flops=0, **options):
    return pl.pallas_call(
        kernel,
        out_shape=[jax.ShapeDtypeStruct(shape, dtype) for shape, dtype in outs],
        scratch_shapes=[pltpu.VMEM(shape, f32) if isinstance(shape, tuple) else shape for shape in scratch],
        compiler_params=pltpu.CompilerParams(vmem_limit_bytes=mebibytes << 20),
        cost_estimate=pl.CostEstimate(flops=flops, bytes_accessed=1 << 10, transcendentals=0),
        **options,
    )


def per_device(
    embedding,
    emb_state,
    entity_slot,
    relations,
    rel_state,
    edge_src,
    edge_rel,
    edge_dst,
    negatives,
    edge_count,
):
    flat = (chips * ent_rows, 128)
    core = (lax.axis_index("blk") % 2).astype(f32).reshape(1, 1)
    embedding, relations = embedding.T, relations.T
    given = (entity_slot.reshape(1, half), embedding, edge_src, edge_rel, edge_dst, negatives, edge_count.T)
    send, perm, edges = call(
        start_kernel,
        [((chips * out_rows, 128), f32), ((half, half), bf16), ((steps * edge_rows, 128), f32)],
        60,
        [pltpu.VMEM(a.shape, a.dtype) for a in given] + [(128, half), pltpu.SemaphoreType.DMA((7,))],
        in_specs=[pl.BlockSpec(memory_space=pltpu.HBM)] * 7,
    )(*given)
    own = exchanged(send)
    here = sent(edges[: 2 * edge_rows], edges_here)
    following = sent(edges[2 * edge_rows :], edges_next)
    own, here, following = lax.optimization_barrier((own, here, following))
    row = ((1, half), f32)
    ops, state, rel_state = call(operator_kernel, [((steps * cap, wide), f32), row, row], 16, [(wide, nrel)])(
        relations, here, following, emb_state.reshape(1, half), rel_state.reshape(1, nrel)
    )
    mate = sent(own, swap_cores)
    rel_flat = ((chips * rel_rows, 128), f32)
    kept = [((2 * cap, part), bf16), ((2 * cap, wide), bf16), ((4 * cap, wide), bf16), ((part, 128), f32)]
    down_keep, down_give, up_keep, up_give, rel_keep, rel_give, *for_own = call(
        unit_kernel, [(flat, f32)] * 4 + [rel_flat] * 2 + kept, 28
    )(own, mate, ops, here, following, core)
    own_keep, own_give = call(own_kernel, [(flat, f32)] * 2, 12, flops=4 << 30)(*for_own, here)
    gives = [sent(give, swap_cores) for give in (up_give, down_give, rel_give)]
    up_sum, down_sum, rel_sum = call(add_kernel, [(flat, f32)] * 2 + [rel_flat], 8)(up_keep, down_keep, rel_keep, *gives)
    own_got = sent(own_give, swap_cores)
    from_up = sent(down_sum, go_down)
    from_down = sent(up_sum, go_up)
    rel_got = exchanged(rel_sum)
    (back,) = call(gather_kernel, [((chips * back_rows, 128), f32)], 16)(own_keep, own_got, from_up, from_down, rel_got)
    got = exchanged(back)
    (rel_own,) = call(rel_half_kernel, [((wide, 128), f32)], 8)(got)
    rel_mate = sent(rel_own, swap_cores)
    new_embedding, new_state = call(entity_kernel, [((width, half), f32), row], 16)(got, perm, embedding, state)
    new_relations, new_rel_state = call(relation_kernel, [((width, nrel), f32), row], 8)(
        rel_own, rel_mate, core, relations, rel_state
    )
    return (
        new_embedding.T,
        new_state.reshape(half),
        new_relations.T,
        new_rel_state.reshape(nrel),
    )


def solution(mesh):
    placed = (
        P(axes, None),
        P(axes),
        P(axes),
        P(),
        P(),
        P(None, axes),
        P(None, axes),
        P(None, axes),
        P(None, axes),
        P(None, axes),
    )
    return jax.shard_map(
        per_device,
        mesh=mesh,
        in_specs=placed,
        out_specs=(P(axes, None), P(axes), P(), P()),
        check_vma=False,
    )
```

```python
import jax
import jax.numpy as jnp
from jax import lax
from jax.experimental import pallas as pl
from jax.experimental.pallas import tpu as pltpu
from jax.sharding import PartitionSpec as P

learn_rate = 0.1
axes = ("blk", "rows")
devices = 128
chips = 64
part = 512
half = 256
width = 400
wide = 512
nrel = 256
cap = 512
nneg = 1000
steps = 3
edge_rows = 24
edge = 384
tail = width - edge
out_rows = 39
ent_rows = 13
rel_rows = 7
back_rows = 19
ent_lanes = (0, 32, 64, 96)
f32 = jnp.float32
bf16 = jnp.bfloat16


def device_at(place, core):
    visit, y, step = place // 32, place // 8 % 4, place % 8
    x = step if step < 4 else 7 - step
    odd = (y % 2) if step < 4 else 1 - y % 2
    z = 2 * visit + odd if y < 3 or odd else (2 * visit + 2) % 4
    block = (((z % 2) * 4 + y) * 4 + x) * 2 + core
    return block * 2 + z // 2


def every(source, target):
    return [(source(p, h), target(p, h)) for p in range(chips) for h in range(2)]


swap_cores = every(device_at, lambda p, h: device_at(p, 1 - h))
go_up = every(device_at, lambda p, h: device_at((p + 1) % chips, h))
go_down = every(device_at, lambda p, h: device_at((p - 1) % chips, h))
edges_next = every(lambda p, h: 2 * ((p + 1) % chips) + h, device_at)
same_core = [[device_at(p, h) for p in range(chips)] for h in range(2)]
edges_here = every(lambda p, h: 2 * p + h, device_at)


def sent(value, pairs):
    return lax.ppermute(value, axes, pairs)


def exchanged(value):
    rows = value.shape[0]
    blocks = value.reshape(chips, rows // chips, 1, 128)
    got = lax.all_to_all(blocks, axes, split_axis=0, concat_axis=0, axis_index_groups=same_core, tiled=True)
    return got.reshape(rows, 128)


def two(value):
    high = value.astype(bf16)
    return high, (value - high.astype(f32)).astype(bf16)


def three(value):
    high = value.astype(bf16)
    rest = value - high.astype(f32)
    mid = rest.astype(bf16)
    return high, mid, (rest - mid.astype(f32)).astype(bf16)


def mm(a, b, contract=(1, 0)):
    return lax.dot_general(
        a, b, (((contract[0],), (contract[1],)), ((), ())), preferred_element_type=f32
    )


def mm3(a, b, contract=(1, 0)):
    return (mm(a[0], b[1], contract) + mm(a[1], b[0], contract)) + mm(a[0], b[0], contract)


def lane_iota(shape):
    return lax.broadcasted_iota(jnp.int32, shape, len(shape) - 1)


def start_kernel(*refs):
    far, (send_ref, perm_ref, edge_ref), near = refs[:7], refs[7:10], refs[10:17]
    last_ref, arrived = refs[17:]
    copies = [pltpu.make_async_copy(a, b, arrived.at[i]) for i, (a, b) in enumerate(zip(far, near))]
    for copy in copies:
        copy.start()
    slot_ref, emb_ref, src_ref, rel_ref, dst_ref, neg_ref, count_ref = near
    copies[0].wait()
    slot = slot_ref[...]
    match = lax.broadcasted_iota(jnp.int32, (chips, half), 0) == slot // part
    before = (
        lax.broadcasted_iota(jnp.int32, (half, half), 0) < lane_iota((half, half))
    ).astype(f32).astype(bf16)
    earlier = mm(match.astype(f32).astype(bf16), before)
    picks = [jnp.where(match, jnp.where(jnp.abs(earlier - layer) < 0.5, 1.0, 0.0), 0.0) for layer in range(4)]
    perm = jnp.concatenate(picks, axis=0).astype(bf16)
    perm_ref[...] = perm
    last_ref[...] = jnp.zeros(last_ref.shape, f32)
    copies[1].wait()
    last_ref[:tail, :] = emb_ref[edge:, :]
    last_ref[tail : tail + 1, :] = (slot & (part - 1)).astype(f32)
    outs = []
    for c in range(4):
        high, mid, low = three(emb_ref[c * 128 : (c + 1) * 128, :] if c < 3 else last_ref[...])
        outs.append(mm(perm, high, (1, 1)) + (mm(perm, mid, (1, 1)) + mm(perm, low, (1, 1))))
    for which, shift in enumerate((0, 1, chips - 1)):
        store_rows(send_ref, outs, 0, 4, out_rows, which * ent_rows, shift)
    for copy in copies[2:]:
        copy.wait()
    for s in range(steps):
        base = s * edge_rows
        for j in range(4):
            lanes = slice(j * 128, (j + 1) * 128)
            edge_ref[base + j : base + j + 1, :] = src_ref[s : s + 1, lanes].astype(f32)
            edge_ref[base + 4 + j : base + 5 + j, :] = rel_ref[s : s + 1, lanes].astype(f32)
            edge_ref[base + 8 + j : base + 9 + j, :] = dst_ref[s : s + 1, lanes].astype(f32)
        edge_ref[base + 19 : base + 20, :] = jnp.full((1, 128), -1.0, f32)
        for j in range(8):
            end = min((j + 1) * 128, nneg)
            edge_ref[base + 12 + j : base + 13 + j, : end - j * 128] = neg_ref[
                s : s + 1, j * 128 : end
            ].astype(f32)
        edge_ref[base + 20 : base + edge_rows, :] = jnp.broadcast_to(
            count_ref[:, s : s + 1].astype(f32), (edge_rows - 20, 128)
        )


def rolled(value, lanes):
    return pltpu.roll(value, lanes, 1) if lanes % 128 else value


def main_and_tails(ref, rows, firsts, lanes, last_row):
    blocks = []
    for c in range(3):
        blocks.append(jnp.concatenate([ref[pl.ds(first + c, chips, stride=rows), :] for first in firsts], axis=0))
    last = ref[pl.ds(last_row, chips, stride=rows), :]
    return blocks + [jnp.concatenate([rolled(last, (128 - lane) % 128) for lane in lanes], axis=0)]


def ent_blocks(ref, rows, base, last_row):
    return main_and_tails(ref, rows, [base + 3 * layer for layer in range(4)], ent_lanes, last_row)


def store_rows(ref, columns, begin, layers, rows=None, base=0, shift=0):
    rows = rows or 3 * layers + 1
    turned = lambda value: pltpu.roll(value, shift, 0) if shift else value
    tails = 0.0
    for layer in range(layers):
        now = slice(begin + layer * chips, begin + (layer + 1) * chips)
        for c in range(3):
            ref[pl.ds(base + layer * 3 + c, chips, stride=rows), :] = turned(columns[c][now, :])
        tails = tails + rolled(columns[3][now, :], ent_lanes[layer])
    ref[pl.ds(base + 3 * layers, chips, stride=rows), :] = turned(tails)


def column_blocks(value):
    return [value[:, c * 128 : (c + 1) * 128] for c in range(4)]


def joined_blocks(blocks):
    last = blocks[3]
    column = last[:, tail : tail + 1]
    row = last.T[tail : tail + 1, :]
    last = jnp.where(lane_iota(last.shape) < tail, last, 0.0)
    return two(jnp.concatenate(blocks[:3] + [last], axis=1)), row, column


def load_half(ref, which):
    base = which * ent_rows
    return joined_blocks(ent_blocks(ref, out_rows, base, base + ent_rows - 1))


def both_halves(own, mate):
    pair = tuple(jnp.concatenate([a, b], axis=0) for a, b in zip(own[0], mate[0]))
    return pair, jnp.concatenate([own[1], mate[1]], axis=1), jnp.concatenate([own[2], mate[2]], axis=0)


def onehot(a, b):
    return jnp.where(a == b, 1.0, 0.0).astype(bf16)


def edge_views(edges):
    flipped = edges.T
    row = lambda first: jnp.concatenate([edges[first + j : first + j + 1, :] for j in range(4)], axis=1)
    column = lambda first, n: jnp.concatenate([flipped[:, first + j : first + j + 1] for j in range(n)], axis=0)
    return row, column


def heads(lhs, edges):
    (high, low), row, _ = lhs
    pick = onehot(edge_views(edges)[1](0, 4), row)
    return mm(pick, low) + mm(pick, high)


def operators(rel, edges):
    high, low = rel
    pick = onehot(edge_views(edges)[1](4, 4), lane_iota((cap, nrel)).astype(f32))
    return mm(pick, low, (1, 1)) + mm(pick, high, (1, 1))


def terms(rhs, head, ops, edge_sets, core):
    rhs_two, rrow, _ = rhs
    row_ids = lax.broadcasted_iota(jnp.int32, (nrel, 1), 0).astype(f32)
    row_ids = jnp.where(core > 0.5, jnp.where(row_ids < nrel // 2, row_ids + nrel // 2, row_ids - nrel // 2), row_ids)
    joined = two(head * ops)
    scores = mm3(joined, rhs_two, (1, 1))
    weights, put_rels = [], []
    for i, edges in enumerate(edge_sets):
        row, column = edge_views(edges)
        at_dst = column(8, 4) == rrow
        times = jnp.sum(jnp.where(column(12, 8) == rrow, 1.0, 0.0), axis=0, keepdims=True) * (1.0 / nneg)
        live = lax.broadcasted_iota(jnp.int32, (cap, 1), 0).astype(f32) < edges[20:21, 0:1]
        score = scores[i * cap : (i + 1) * cap, :]
        pos = jnp.sum(jnp.where(at_dst, score, 0.0), axis=1, keepdims=True)
        weight = times * (0.5 + 0.5 * jnp.tanh(0.5 * score)) - jnp.where(at_dst, jax.nn.sigmoid(-pos), 0.0)
        weights.append(jnp.where(live, weight, 0.0))
        put_rels.append(onehot(row_ids, row(4)))
    weight = two(jnp.concatenate(weights, axis=0))
    g_joined = mm3(weight, rhs_two)
    gh, gl = two(g_joined * head)
    put_rel = jnp.concatenate(put_rels, axis=1)
    rel_grad = mm(put_rel, gl) + mm(put_rel, gh)
    return weight, joined, two(g_joined * ops), rel_grad


def put_back(lcol, edges, grads):
    put_src = onehot(lcol, edge_views(edges)[0](0))
    return mm(put_src, grads[1]) + mm(put_src, grads[0])


def load_rel(rel_ref, pad_ref):
    pad_ref[384:, :] = jnp.zeros((128, nrel), f32)
    pad_ref[:width, :] = rel_ref[...]
    return two(pad_ref[...])


def store_half(ref, grad, which):
    store_rows(ref, column_blocks(grad), which * half, 4)


def operator_kernel(
    own_ref, rel_ref, edge_ref, next_ref, state_ref, rel_state_ref, ops_ref, head_ref, state_out, rel_state_out, pad_ref
):
    mine, above = load_half(own_ref, 0), load_half(own_ref, 2)
    rel = load_rel(rel_ref, pad_ref)
    sets = (edge_ref[:edge_rows, :], edge_ref[edge_rows : 2 * edge_rows, :], next_ref[...])
    for i, edges in enumerate(sets):
        ops_ref[i * cap : (i + 1) * cap, :] = operators(rel, edges)
        head_ref[i * cap : (i + 1) * cap, :] = heads(mine if i < 2 else above, edges)
    state_out[...] = state_ref[...]
    rel_state_out[...] = rel_state_ref[...]


def unit_kernel(
    own_ref, mate_ref, ops_ref, head_ref, edge_ref, next_ref, core_ref,
    down_keep, down_give, up_keep, up_give, rel_keep, rel_give, weight_ref, joined_ref, head_grad_ref, place_ref,
):
    mates = [load_half(mate_ref, which) for which in range(3)]
    mine, below = [both_halves(load_half(own_ref, which), mates[which]) for which in range(2)]
    own_last, mate_last = [ent_blocks(ref, out_rows, 2 * ent_rows, out_rows - 1)[3] for ref in (own_ref, mate_ref)]
    above_places = jnp.concatenate([own_last, mate_last], axis=0)[:, tail : tail + 1]
    core = core_ref[...]
    first, now, later = edge_ref[:edge_rows, :], edge_ref[edge_rows : 2 * edge_rows, :], next_ref[...]
    weight, joined, grads, rel0 = terms(mine, head_ref[:cap, :] + heads(mates[0], first), ops_ref[:cap, :], [first], core)
    for i in range(2):
        weight_ref[i * cap : (i + 1) * cap, :] = weight[i]
        joined_ref[i * cap : (i + 1) * cap, :] = joined[i]
        head_grad_ref[i * cap : (i + 1) * cap, :] = grads[i]
    head = head_ref[cap:, :] + jnp.concatenate([heads(mates[0], now), heads(mates[2], later)], axis=0)
    weight, joined, grads, relg = terms(below, head, ops_ref[cap:, :], [now, later], core)
    for i in range(2):
        head_grad_ref[(i + 2) * cap : (i + 3) * cap, :] = grads[i][:cap, :]
    place_ref[...] = jnp.broadcast_to(mine[2], (part, 128))
    dg = mm3(weight, joined, (0, 0))
    ug = put_back(above_places, later, (grads[0][cap:, :], grads[1][cap:, :]))
    relg = relg + rel0
    store_half(up_keep, ug, 0)
    store_half(up_give, ug, 1)
    store_half(down_keep, dg, 0)
    store_half(down_give, dg, 1)
    store_rows(rel_keep, column_blocks(relg), 0, 2)
    store_rows(rel_give, column_blocks(relg), nrel // 2, 2)


def own_kernel(weight_ref, joined_ref, head_grad_ref, place_ref, edge_ref, own_keep, own_give):
    pair = lambda ref, i: (ref[i * cap : (i + 1) * cap, :], ref[(i + 1) * cap : (i + 2) * cap, :])
    places = place_ref[:, 0:1]
    lg = mm3(pair(weight_ref, 0), pair(joined_ref, 0), (0, 0))
    lg = lg + put_back(places, edge_ref[:edge_rows, :], pair(head_grad_ref, 0))
    lg = lg + put_back(places, edge_ref[edge_rows : 2 * edge_rows, :], pair(head_grad_ref, 2))
    store_half(own_keep, lg, 0)
    store_half(own_give, lg, 1)


def add_kernel(*refs):
    for a, b, out in zip(refs[:3], refs[3:6], refs[6:]):
        out[...] = a[...] + b[...]


def gather_kernel(keep_ref, give_ref, up_ref, down_ref, rel_ref, out_ref):
    for j in range(ent_rows):
        rows = pl.ds(j, chips, stride=ent_rows)
        sums = (keep_ref[rows, :] + give_ref[rows, :]) + (up_ref[rows, :] + down_ref[rows, :])
        if j < ent_rows - 1:
            out_ref[pl.ds(j, chips, stride=back_rows), :] = sums
    for j in range(rel_rows):
        rel = jnp.sum(rel_ref[pl.ds(j, chips, stride=rel_rows), :], axis=0, keepdims=True)
        rel = jnp.broadcast_to(rel, (chips, 128))
        if j < rel_rows - 1:
            out_ref[pl.ds(ent_rows - 1 + j, chips, stride=back_rows), :] = rel
        else:
            out_ref[pl.ds(back_rows - 1, chips, stride=back_rows), :] = sums + rolled(rel, tail)


def update(grads, value_ref, state_ref, new_value_ref, new_state_ref):
    state = state_ref[...] + sum(jnp.sum(g * g, axis=0, keepdims=True) for g in grads) * (1.0 / width)
    new_state_ref[...] = state
    scale = learn_rate / jnp.sqrt(state)
    for c in range(4):
        begin, end = c * 128, min((c + 1) * 128, width)
        new_value_ref[begin:end, :] = value_ref[begin:end, :] - scale * grads[c][: end - begin, :]


def rel_half_kernel(got_ref, out_ref):
    blocks = main_and_tails(got_ref, back_rows, (12, 15), (tail, 32 + tail), back_rows - 1)
    for c in range(4):
        rows = blocks[c] if c < 3 else jnp.where(lane_iota(blocks[c].shape) < tail, blocks[c], 0.0)
        out_ref[c * 128 : (c + 1) * 128, :] = rows


def entity_kernel(got_ref, perm_ref, emb_ref, state_ref, new_emb_ref, new_state_ref):
    perm = perm_ref[...]
    grads = []
    for c, rows in enumerate(ent_blocks(got_ref, back_rows, 0, back_rows - 1)):
        if c == 3:
            rows = jnp.where(lane_iota(rows.shape) < tail, rows, 0.0)
        high, mid, low = three(rows)
        grads.append(mm(high, perm, (0, 0)) + (mm(mid, perm, (0, 0)) + mm(low, perm, (0, 0))))
    update(grads, emb_ref, state_ref, new_emb_ref, new_state_ref)


def relation_kernel(own_ref, mate_ref, core_ref, rel_ref, rel_state_ref, new_rel_ref, new_rel_state_ref):
    first = core_ref[...] < 0.5
    grads = []
    for c in range(4):
        own, mate = own_ref[c * 128 : (c + 1) * 128, :].T, mate_ref[c * 128 : (c + 1) * 128, :].T
        grads.append(jnp.concatenate([jnp.where(first, own, mate), jnp.where(first, mate, own)], axis=1))
    update(grads, rel_ref, rel_state_ref, new_rel_ref, new_rel_state_ref)


def call(kernel, outs, mebibytes, scratch=(), flops=0, **options):
    return pl.pallas_call(
        kernel,
        out_shape=[jax.ShapeDtypeStruct(shape, dtype) for shape, dtype in outs],
        scratch_shapes=[pltpu.VMEM(shape, f32) if isinstance(shape, tuple) else shape for shape in scratch],
        compiler_params=pltpu.CompilerParams(vmem_limit_bytes=mebibytes << 20),
        cost_estimate=pl.CostEstimate(flops=flops, bytes_accessed=1 << 10, transcendentals=0),
        **options,
    )


def per_device(
    embedding,
    emb_state,
    entity_slot,
    relations,
    rel_state,
    edge_src,
    edge_rel,
    edge_dst,
    negatives,
    edge_count,
):
    flat = (chips * ent_rows, 128)
    core = (lax.axis_index("blk") % 2).astype(f32).reshape(1, 1)
    embedding, relations = embedding.T, relations.T
    given = (entity_slot.reshape(1, half), embedding, edge_src, edge_rel, edge_dst, negatives, edge_count.T)
    send, perm, edges = call(
        start_kernel,
        [((chips * out_rows, 128), f32), ((half, half), bf16), ((steps * edge_rows, 128), f32)],
        60,
        [pltpu.VMEM(a.shape, a.dtype) for a in given] + [(128, half), pltpu.SemaphoreType.DMA((7,))],
        in_specs=[pl.BlockSpec(memory_space=pltpu.HBM)] * 7,
    )(*given)
    own = exchanged(send)
    here = sent(edges[: 2 * edge_rows], edges_here)
    following = sent(edges[2 * edge_rows :], edges_next)
    own, here, following = lax.optimization_barrier((own, here, following))
    row = ((1, half), f32)
    ops, head, state, rel_state = call(
        operator_kernel, [((steps * cap, wide), f32)] * 2 + [row, row], 12, [(wide, nrel)]
    )(
        own, relations, here, following, emb_state.reshape(1, half), rel_state.reshape(1, nrel)
    )
    mate = sent(own, swap_cores)
    rel_flat = ((chips * rel_rows, 128), f32)
    kept = [((2 * cap, part), bf16), ((2 * cap, wide), bf16), ((4 * cap, wide), bf16), ((part, 128), f32)]
    down_keep, down_give, up_keep, up_give, rel_keep, rel_give, *for_own = call(
        unit_kernel, [(flat, f32)] * 4 + [rel_flat] * 2 + kept, 28
    )(own, mate, ops, head, here, following, core)
    own_keep, own_give = call(own_kernel, [(flat, f32)] * 2, 12, flops=4 << 30)(*for_own, here)
    gives = [sent(give, swap_cores) for give in (up_give, down_give, rel_give)]
    up_sum, down_sum, rel_sum = call(add_kernel, [(flat, f32)] * 2 + [rel_flat], 8)(up_keep, down_keep, rel_keep, *gives)
    own_got = sent(own_give, swap_cores)
    from_up = sent(down_sum, go_down)
    from_down = sent(up_sum, go_up)
    rel_sum, own_got = lax.optimization_barrier((rel_sum, own_got))
    rel_got = exchanged(rel_sum)
    (back,) = call(gather_kernel, [((chips * back_rows, 128), f32)], 16)(own_keep, own_got, from_up, from_down, rel_got)
    got = exchanged(back)
    (rel_own,) = call(rel_half_kernel, [((wide, 128), f32)], 8)(got)
    rel_mate = sent(rel_own, swap_cores)
    new_embedding, new_state = call(entity_kernel, [((width, half), f32), row], 16)(got, perm, embedding, state)
    new_relations, new_rel_state = call(relation_kernel, [((width, nrel), f32), row], 8)(
        rel_own, rel_mate, core, relations, rel_state
    )
    return (
        new_embedding.T,
        new_state.reshape(half),
        new_relations.T,
        new_rel_state.reshape(nrel),
    )


def solution(mesh):
    placed = (
        P(axes, None),
        P(axes),
        P(axes),
        P(),
        P(),
        P(None, axes),
        P(None, axes),
        P(None, axes),
        P(None, axes),
        P(None, axes),
    )
    return jax.shard_map(
        per_device,
        mesh=mesh,
        in_specs=placed,
        out_specs=(P(axes, None), P(axes), P(), P()),
        check_vma=False,
    )
```

```python
import jax
import jax.numpy as jnp
from jax import lax
from jax.experimental import pallas as pl
from jax.experimental.pallas import tpu as pltpu
from jax.sharding import PartitionSpec as P

learn_rate = 0.1
axes = ("blk", "rows")
devices = 128
chips = 64
part = 512
half = 256
width = 400
wide = 512
nrel = 256
cap = 512
nneg = 1000
steps = 3
edge_rows = 24
edge = 384
tail = width - edge
out_rows = 39
ent_rows = 13
rel_rows = 7
back_rows = 19
ent_lanes = (0, 32, 64, 96)
f32 = jnp.float32
bf16 = jnp.bfloat16


def device_at(place, core):
    visit, y, step = place // 32, place // 8 % 4, place % 8
    x = step if step < 4 else 7 - step
    odd = (y % 2) if step < 4 else 1 - y % 2
    z = 2 * visit + odd if y < 3 or odd else (2 * visit + 2) % 4
    block = (((z % 2) * 4 + y) * 4 + x) * 2 + core
    return block * 2 + z // 2


def every(source, target):
    return [(source(p, h), target(p, h)) for p in range(chips) for h in range(2)]


swap_cores = every(device_at, lambda p, h: device_at(p, 1 - h))
go_up = every(device_at, lambda p, h: device_at((p + 1) % chips, h))
go_down = every(device_at, lambda p, h: device_at((p - 1) % chips, h))
edges_next = every(lambda p, h: 2 * ((p + 1) % chips) + h, device_at)
same_core = [[device_at(p, h) for p in range(chips)] for h in range(2)]
edges_here = every(lambda p, h: 2 * p + h, device_at)


def sent(value, pairs):
    return lax.ppermute(value, axes, pairs)


def exchanged(value):
    rows = value.shape[0]
    blocks = value.reshape(chips, rows // chips, 1, 128)
    got = lax.all_to_all(blocks, axes, split_axis=0, concat_axis=0, axis_index_groups=same_core, tiled=True)
    return got.reshape(rows, 128)


def two(value):
    high = value.astype(bf16)
    return high, (value - high.astype(f32)).astype(bf16)


def three(value):
    high = value.astype(bf16)
    rest = value - high.astype(f32)
    mid = rest.astype(bf16)
    return high, mid, (rest - mid.astype(f32)).astype(bf16)


def mm(a, b, contract=(1, 0)):
    return lax.dot_general(
        a, b, (((contract[0],), (contract[1],)), ((), ())), preferred_element_type=f32
    )


def mm3(a, b, contract=(1, 0)):
    left = jnp.concatenate([a[0], a[1], a[0]], axis=contract[0])
    right = jnp.concatenate([b[1], b[0], b[0]], axis=contract[1])
    return mm(left, right, contract)


def mm2(a, b, contract=(1, 0)):
    left = jnp.concatenate([a, a], axis=contract[0])
    right = jnp.concatenate([b[1], b[0]], axis=contract[1])
    return mm(left, right, contract)


def lane_iota(shape):
    return lax.broadcasted_iota(jnp.int32, shape, len(shape) - 1)


def start_kernel(*refs):
    far, (send_ref, perm_ref, edge_ref), near = refs[:7], refs[7:10], refs[10:17]
    last_ref, arrived = refs[17:]
    copies = [pltpu.make_async_copy(a, b, arrived.at[i]) for i, (a, b) in enumerate(zip(far, near))]
    for copy in copies:
        copy.start()
    slot_ref, emb_ref, src_ref, rel_ref, dst_ref, neg_ref, count_ref = near
    copies[0].wait()
    slot = slot_ref[...]
    match = lax.broadcasted_iota(jnp.int32, (chips, half), 0) == slot // part
    before = (
        lax.broadcasted_iota(jnp.int32, (half, half), 0) < lane_iota((half, half))
    ).astype(f32).astype(bf16)
    earlier = mm(match.astype(f32).astype(bf16), before)
    picks = [jnp.where(match, jnp.where(jnp.abs(earlier - layer) < 0.5, 1.0, 0.0), 0.0) for layer in range(4)]
    perm = jnp.concatenate(picks, axis=0).astype(bf16)
    perm_ref[...] = perm
    last_ref[...] = jnp.zeros(last_ref.shape, f32)
    copies[1].wait()
    last_ref[:tail, :] = emb_ref[edge:, :]
    last_ref[tail : tail + 1, :] = (slot & (part - 1)).astype(f32)
    outs = []
    for c in range(4):
        high, mid, low = three(emb_ref[c * 128 : (c + 1) * 128, :] if c < 3 else last_ref[...])
        outs.append(mm(perm, high, (1, 1)) + (mm(perm, mid, (1, 1)) + mm(perm, low, (1, 1))))
    for which, shift in enumerate((0, 1, chips - 1)):
        store_rows(send_ref, outs, 0, 4, out_rows, which * ent_rows, shift)
    for copy in copies[2:]:
        copy.wait()
    for s in range(steps):
        base = s * edge_rows
        for j in range(4):
            lanes = slice(j * 128, (j + 1) * 128)
            edge_ref[base + j : base + j + 1, :] = src_ref[s : s + 1, lanes].astype(f32)
            edge_ref[base + 4 + j : base + 5 + j, :] = rel_ref[s : s + 1, lanes].astype(f32)
            edge_ref[base + 8 + j : base + 9 + j, :] = dst_ref[s : s + 1, lanes].astype(f32)
        edge_ref[base + 19 : base + 20, :] = jnp.full((1, 128), -1.0, f32)
        for j in range(8):
            end = min((j + 1) * 128, nneg)
            edge_ref[base + 12 + j : base + 13 + j, : end - j * 128] = neg_ref[
                s : s + 1, j * 128 : end
            ].astype(f32)
        edge_ref[base + 20 : base + edge_rows, :] = jnp.broadcast_to(
            count_ref[:, s : s + 1].astype(f32), (edge_rows - 20, 128)
        )


def rolled(value, lanes):
    return pltpu.roll(value, lanes, 1) if lanes % 128 else value


def main_and_tails(ref, rows, firsts, lanes, last_row):
    blocks = []
    for c in range(3):
        blocks.append(jnp.concatenate([ref[pl.ds(first + c, chips, stride=rows), :] for first in firsts], axis=0))
    last = ref[pl.ds(last_row, chips, stride=rows), :]
    return blocks + [jnp.concatenate([rolled(last, (128 - lane) % 128) for lane in lanes], axis=0)]


def ent_blocks(ref, rows, base, last_row):
    return main_and_tails(ref, rows, [base + 3 * layer for layer in range(4)], ent_lanes, last_row)


def store_rows(ref, columns, begin, layers, rows=None, base=0, shift=0):
    rows = rows or 3 * layers + 1
    turned = lambda value: pltpu.roll(value, shift, 0) if shift else value
    tails = 0.0
    for layer in range(layers):
        now = slice(begin + layer * chips, begin + (layer + 1) * chips)
        for c in range(3):
            ref[pl.ds(base + layer * 3 + c, chips, stride=rows), :] = turned(columns[c][now, :])
        tails = tails + rolled(columns[3][now, :], ent_lanes[layer])
    ref[pl.ds(base + 3 * layers, chips, stride=rows), :] = turned(tails)


def column_blocks(value):
    return [value[:, c * 128 : (c + 1) * 128] for c in range(4)]


def joined_blocks(blocks):
    last = blocks[3]
    column = last[:, tail : tail + 1]
    row = last.T[tail : tail + 1, :]
    last = jnp.where(lane_iota(last.shape) < tail, last, 0.0)
    return two(jnp.concatenate(blocks[:3] + [last], axis=1)), row, column


def load_half(ref, which):
    base = which * ent_rows
    return joined_blocks(ent_blocks(ref, out_rows, base, base + ent_rows - 1))


def both_halves(own, mate):
    pair = tuple(jnp.concatenate([a, b], axis=0) for a, b in zip(own[0], mate[0]))
    return pair, jnp.concatenate([own[1], mate[1]], axis=1), jnp.concatenate([own[2], mate[2]], axis=0)


def onehot(a, b):
    return jnp.where(a == b, 1.0, 0.0).astype(bf16)


def edge_views(edges):
    flipped = edges.T
    row = lambda first: jnp.concatenate([edges[first + j : first + j + 1, :] for j in range(4)], axis=1)
    column = lambda first, n: jnp.concatenate([flipped[:, first + j : first + j + 1] for j in range(n)], axis=0)
    return row, column


def heads(lhs, edges):
    (high, low), row, _ = lhs
    pick = onehot(edge_views(edges)[1](0, 4), row)
    return mm2(pick, (high, low))


def operators(rel, edges):
    high, low = rel
    pick = onehot(edge_views(edges)[1](4, 4), lane_iota((cap, nrel)).astype(f32))
    return mm2(pick, (high, low), (1, 1))


def terms(rhs, head, ops, edge_sets, core):
    rhs_two, rrow, _ = rhs
    row_ids = lax.broadcasted_iota(jnp.int32, (nrel, 1), 0).astype(f32)
    row_ids = jnp.where(core > 0.5, jnp.where(row_ids < nrel // 2, row_ids + nrel // 2, row_ids - nrel // 2), row_ids)
    joined = two(head * ops)
    scores = mm3(joined, rhs_two, (1, 1))
    weights, put_rels = [], []
    for i, edges in enumerate(edge_sets):
        row, column = edge_views(edges)
        at_dst = column(8, 4) == rrow
        times = jnp.sum(jnp.where(column(12, 8) == rrow, 1.0, 0.0), axis=0, keepdims=True) * (1.0 / nneg)
        live = lax.broadcasted_iota(jnp.int32, (cap, 1), 0).astype(f32) < edges[20:21, 0:1]
        score = scores[i * cap : (i + 1) * cap, :]
        pos = jnp.sum(jnp.where(at_dst, score, 0.0), axis=1, keepdims=True)
        weight = times * (0.5 + 0.5 * jnp.tanh(0.5 * score)) - jnp.where(at_dst, jax.nn.sigmoid(-pos), 0.0)
        weights.append(jnp.where(live, weight, 0.0))
        put_rels.append(onehot(row_ids, row(4)))
    weight = two(jnp.concatenate(weights, axis=0))
    g_joined = mm3(weight, rhs_two)
    gh, gl = two(g_joined * head)
    put_rel = jnp.concatenate(put_rels, axis=1)
    rel_grad = mm2(put_rel, (gh, gl))
    return weight, joined, two(g_joined * ops), rel_grad


def put_back(lcol, edges, grads):
    put_src = onehot(lcol, edge_views(edges)[0](0))
    return mm2(put_src, grads)


def load_rel(rel_ref, pad_ref):
    pad_ref[384:, :] = jnp.zeros((128, nrel), f32)
    pad_ref[:width, :] = rel_ref[...]
    return two(pad_ref[...])


def store_half(ref, grad, which):
    store_rows(ref, column_blocks(grad), which * half, 4)


def operator_kernel(
    own_ref, rel_ref, edge_ref, next_ref, state_ref, rel_state_ref, ops_ref, head_ref, state_out, rel_state_out, pad_ref
):
    mine, above = load_half(own_ref, 0), load_half(own_ref, 2)
    rel = load_rel(rel_ref, pad_ref)
    sets = (edge_ref[:edge_rows, :], edge_ref[edge_rows : 2 * edge_rows, :], next_ref[...])
    for i, edges in enumerate(sets):
        ops_ref[i * cap : (i + 1) * cap, :] = operators(rel, edges)
        head_ref[i * cap : (i + 1) * cap, :] = heads(mine if i < 2 else above, edges)
    state_out[...] = state_ref[...]
    rel_state_out[...] = rel_state_ref[...]


def unit_kernel(
    own_ref, mate_ref, ops_ref, head_ref, edge_ref, next_ref, core_ref,
    down_keep, down_give, up_keep, up_give, rel_keep, rel_give, weight_ref, joined_ref, head_grad_ref, place_ref,
):
    mates = [load_half(mate_ref, which) for which in range(3)]
    mine, below = [both_halves(load_half(own_ref, which), mates[which]) for which in range(2)]
    own_last, mate_last = [ent_blocks(ref, out_rows, 2 * ent_rows, out_rows - 1)[3] for ref in (own_ref, mate_ref)]
    above_places = jnp.concatenate([own_last, mate_last], axis=0)[:, tail : tail + 1]
    core = core_ref[...]
    first, now, later = edge_ref[:edge_rows, :], edge_ref[edge_rows : 2 * edge_rows, :], next_ref[...]
    weight, joined, grads, rel0 = terms(mine, head_ref[:cap, :] + heads(mates[0], first), ops_ref[:cap, :], [first], core)
    for i in range(2):
        weight_ref[i * cap : (i + 1) * cap, :] = weight[i]
        joined_ref[i * cap : (i + 1) * cap, :] = joined[i]
        head_grad_ref[i * cap : (i + 1) * cap, :] = grads[i]
    head = head_ref[cap:, :] + jnp.concatenate([heads(mates[0], now), heads(mates[2], later)], axis=0)
    weight, joined, grads, relg = terms(below, head, ops_ref[cap:, :], [now, later], core)
    for i in range(2):
        head_grad_ref[(i + 2) * cap : (i + 3) * cap, :] = grads[i][:cap, :]
    place_ref[...] = jnp.broadcast_to(mine[2], (part, 128))
    dg = mm3(weight, joined, (0, 0))
    ug = put_back(above_places, later, (grads[0][cap:, :], grads[1][cap:, :]))
    relg = relg + rel0
    store_half(up_keep, ug, 0)
    store_half(up_give, ug, 1)
    store_half(down_keep, dg, 0)
    store_half(down_give, dg, 1)
    store_rows(rel_keep, column_blocks(relg), 0, 2)
    store_rows(rel_give, column_blocks(relg), nrel // 2, 2)


def own_kernel(weight_ref, joined_ref, head_grad_ref, place_ref, edge_ref, own_keep, own_give):
    pair = lambda ref, i: (ref[i * cap : (i + 1) * cap, :], ref[(i + 1) * cap : (i + 2) * cap, :])
    places = place_ref[:, 0:1]
    lg = mm3(pair(weight_ref, 0), pair(joined_ref, 0), (0, 0))
    lg = lg + put_back(places, edge_ref[:edge_rows, :], pair(head_grad_ref, 0))
    lg = lg + put_back(places, edge_ref[edge_rows : 2 * edge_rows, :], pair(head_grad_ref, 2))
    store_half(own_keep, lg, 0)
    store_half(own_give, lg, 1)


def add_kernel(*refs):
    for a, b, out in zip(refs[:3], refs[3:6], refs[6:]):
        out[...] = a[...] + b[...]


def gather_kernel(keep_ref, give_ref, up_ref, down_ref, rel_ref, out_ref):
    for j in range(ent_rows):
        rows = pl.ds(j, chips, stride=ent_rows)
        sums = (keep_ref[rows, :] + give_ref[rows, :]) + (up_ref[rows, :] + down_ref[rows, :])
        if j < ent_rows - 1:
            out_ref[pl.ds(j, chips, stride=back_rows), :] = sums
    for j in range(rel_rows):
        rel = jnp.sum(rel_ref[pl.ds(j, chips, stride=rel_rows), :], axis=0, keepdims=True)
        rel = jnp.broadcast_to(rel, (chips, 128))
        if j < rel_rows - 1:
            out_ref[pl.ds(ent_rows - 1 + j, chips, stride=back_rows), :] = rel
        else:
            out_ref[pl.ds(back_rows - 1, chips, stride=back_rows), :] = sums + rolled(rel, tail)


def update(grads, value_ref, state_ref, new_value_ref, new_state_ref):
    state = state_ref[...] + sum(jnp.sum(g * g, axis=0, keepdims=True) for g in grads) * (1.0 / width)
    new_state_ref[...] = state
    scale = learn_rate / jnp.sqrt(state)
    for c in range(4):
        begin, end = c * 128, min((c + 1) * 128, width)
        new_value_ref[begin:end, :] = value_ref[begin:end, :] - scale * grads[c][: end - begin, :]


def rel_half_kernel(got_ref, out_ref):
    blocks = main_and_tails(got_ref, back_rows, (12, 15), (tail, 32 + tail), back_rows - 1)
    for c in range(4):
        rows = blocks[c] if c < 3 else jnp.where(lane_iota(blocks[c].shape) < tail, blocks[c], 0.0)
        out_ref[c * 128 : (c + 1) * 128, :] = rows


def entity_kernel(got_ref, perm_ref, emb_ref, state_ref, new_emb_ref, new_state_ref):
    perm = perm_ref[...]
    grads = []
    for c, rows in enumerate(ent_blocks(got_ref, back_rows, 0, back_rows - 1)):
        if c == 3:
            rows = jnp.where(lane_iota(rows.shape) < tail, rows, 0.0)
        high, mid, low = three(rows)
        grads.append(mm(high, perm, (0, 0)) + (mm(mid, perm, (0, 0)) + mm(low, perm, (0, 0))))
    update(grads, emb_ref, state_ref, new_emb_ref, new_state_ref)


def relation_kernel(own_ref, mate_ref, core_ref, rel_ref, rel_state_ref, new_rel_ref, new_rel_state_ref):
    first = core_ref[...] < 0.5
    grads = []
    for c in range(4):
        own, mate = own_ref[c * 128 : (c + 1) * 128, :].T, mate_ref[c * 128 : (c + 1) * 128, :].T
        grads.append(jnp.concatenate([jnp.where(first, own, mate), jnp.where(first, mate, own)], axis=1))
    update(grads, rel_ref, rel_state_ref, new_rel_ref, new_rel_state_ref)


def call(kernel, outs, mebibytes, scratch=(), flops=0, **options):
    return pl.pallas_call(
        kernel,
        out_shape=[jax.ShapeDtypeStruct(shape, dtype) for shape, dtype in outs],
        scratch_shapes=[pltpu.VMEM(shape, f32) if isinstance(shape, tuple) else shape for shape in scratch],
        compiler_params=pltpu.CompilerParams(vmem_limit_bytes=mebibytes << 20),
        cost_estimate=pl.CostEstimate(flops=flops, bytes_accessed=1 << 10, transcendentals=0),
        **options,
    )


def per_device(
    embedding,
    emb_state,
    entity_slot,
    relations,
    rel_state,
    edge_src,
    edge_rel,
    edge_dst,
    negatives,
    edge_count,
):
    flat = (chips * ent_rows, 128)
    core = (lax.axis_index("blk") % 2).astype(f32).reshape(1, 1)
    embedding, relations = embedding.T, relations.T
    given = (entity_slot.reshape(1, half), embedding, edge_src, edge_rel, edge_dst, negatives, edge_count.T)
    send, perm, edges = call(
        start_kernel,
        [((chips * out_rows, 128), f32), ((half, half), bf16), ((steps * edge_rows, 128), f32)],
        60,
        [pltpu.VMEM(a.shape, a.dtype) for a in given] + [(128, half), pltpu.SemaphoreType.DMA((7,))],
        in_specs=[pl.BlockSpec(memory_space=pltpu.HBM)] * 7,
    )(*given)
    own = exchanged(send)
    here = sent(edges[: 2 * edge_rows], edges_here)
    following = sent(edges[2 * edge_rows :], edges_next)
    own, here, following = lax.optimization_barrier((own, here, following))
    row = ((1, half), f32)
    ops, head, state, rel_state = call(
        operator_kernel, [((steps * cap, wide), f32)] * 2 + [row, row], 12, [(wide, nrel)]
    )(
        own, relations, here, following, emb_state.reshape(1, half), rel_state.reshape(1, nrel)
    )
    mate = sent(own, swap_cores)
    rel_flat = ((chips * rel_rows, 128), f32)
    kept = [((2 * cap, part), bf16), ((2 * cap, wide), bf16), ((4 * cap, wide), bf16), ((part, 128), f32)]
    down_keep, down_give, up_keep, up_give, rel_keep, rel_give, *for_own = call(
        unit_kernel, [(flat, f32)] * 4 + [rel_flat] * 2 + kept, 28
    )(own, mate, ops, head, here, following, core)
    own_keep, own_give = call(own_kernel, [(flat, f32)] * 2, 12, flops=4 << 30)(*for_own, here)
    gives = [sent(give, swap_cores) for give in (up_give, down_give, rel_give)]
    up_sum, down_sum, rel_sum = call(add_kernel, [(flat, f32)] * 2 + [rel_flat], 8)(up_keep, down_keep, rel_keep, *gives)
    own_got = sent(own_give, swap_cores)
    from_up = sent(down_sum, go_down)
    from_down = sent(up_sum, go_up)
    rel_sum, own_got = lax.optimization_barrier((rel_sum, own_got))
    rel_got = exchanged(rel_sum)
    (back,) = call(gather_kernel, [((chips * back_rows, 128), f32)], 16)(own_keep, own_got, from_up, from_down, rel_got)
    got = exchanged(back)
    (rel_own,) = call(rel_half_kernel, [((wide, 128), f32)], 8)(got)
    rel_mate = sent(rel_own, swap_cores)
    new_embedding, new_state = call(entity_kernel, [((width, half), f32), row], 16)(got, perm, embedding, state)
    new_relations, new_rel_state = call(relation_kernel, [((width, nrel), f32), row], 8)(
        rel_own, rel_mate, core, relations, rel_state
    )
    return (
        new_embedding.T,
        new_state.reshape(half),
        new_relations.T,
        new_rel_state.reshape(nrel),
    )


def solution(mesh):
    placed = (
        P(axes, None),
        P(axes),
        P(axes),
        P(),
        P(),
        P(None, axes),
        P(None, axes),
        P(None, axes),
        P(None, axes),
        P(None, axes),
    )
    return jax.shard_map(
        per_device,
        mesh=mesh,
        in_specs=placed,
        out_specs=(P(axes, None), P(axes), P(), P()),
        check_vma=False,
    )
```
